512 devices in a mesh: rows: 128 (over z_lo, y, x, core), cols: 4 (over z_hi).
Axes of the slice: x: 4, y: 4, z: 16 (z_hi: 4, z_lo: 4; z = z_hi * 4 + z_lo), core: 2. Of those that a mesh axis runs over, the one named last changes fastest.
Arguments:
- solves: float32 [64, 524288], P('cols', 'rows'), may hold values from -6 to 6
- factor3: float32 [64, 524288], P('cols', 'rows')
- factor2: float32 [64, 524288], P('cols', 'rows')
- factor1: float32 [64, 524288], P('cols', 'rows')
- basis3: float32 [64, 524288], P(None, 'rows')
- basis2: float32 [64, 524288], P(None, 'rows')
- basis1: float32 [64, 524288], P(None, 'rows')
Outputs:
- solution: float32 [64, 524288], P('cols', 'rows')
The draws below stay inside these ranges and needn't reach their ends.
All inputs are finite; a program needn't handle non-finite values.
Results may differ from the reference program's by a relative error of at most 0.000053.
Values sent between devices are 32-bit elements; how exact they have to be, the bound alone decides.
No kernel may reach another device: no remote copies, remote signals or barrier semaphores. Data moves between devices by JAX's collectives and lax.ppermute only.
A program may use at most 64 MiB of HBM per device.

```python
import jax
import jax.numpy as jnp
from jax import lax

RANK = 64
NRHS = 64
ALL_ROWS = 524288
LEAF_ROWS = 65536


def draw_basis3(key, part):
    key = jax.random.fold_in(key, 3)
    scale = 0.3 / jnp.sqrt(1.0 * RANK * LEAF_ROWS)
    values = jnp.clip(jax.random.normal(key, (RANK, ALL_ROWS)), -5.0, 5.0)
    return (scale * values).astype(jnp.float32)


def draw_basis2(key, part):
    key = jax.random.fold_in(key, 5)
    scale = 0.3 / jnp.sqrt(2.0 * RANK * LEAF_ROWS)
    values = jnp.clip(jax.random.normal(key, (RANK, ALL_ROWS)), -5.0, 5.0)
    return (scale * values).astype(jnp.float32)


def draw_basis1(key, part):
    key = jax.random.fold_in(key, 7)
    scale = 0.3 / jnp.sqrt(4.0 * RANK * LEAF_ROWS)
    values = jnp.clip(jax.random.normal(key, (RANK, ALL_ROWS)), -5.0, 5.0)
    return (scale * values).astype(jnp.float32)


def draw_factor3(key, part):
    key = jax.random.fold_in(key, 13)
    values = jnp.clip(jax.random.normal(key, (RANK, ALL_ROWS)), -5.0, 5.0)
    return values.astype(jnp.float32)


def draw_factor2(key, part):
    key = jax.random.fold_in(key, 12)
    values = jnp.clip(jax.random.normal(key, (RANK, ALL_ROWS)), -5.0, 5.0)
    return values.astype(jnp.float32)


def draw_factor1(key, part):
    key = jax.random.fold_in(key, 11)
    values = jnp.clip(jax.random.normal(key, (RANK, ALL_ROWS)), -5.0, 5.0)
    return values.astype(jnp.float32)


def block_levels(stream_key, extent, shards, low, largest):
    loudness = 1.0
    for position, blocks in shards:
        heights = jax.random.uniform(jax.random.fold_in(jax.random.fold_in(stream_key, 6), position), (blocks,), jnp.float32, low / len(shards), largest / len(shards))
        loudness = loudness * jnp.repeat(jnp.exp(heights), extent[position] // blocks).reshape((-1,) + (1,) * (len(extent) - 1 - position))
    return loudness


def noise(key, extent, deviation, reach, pieces=(), kind=jnp.bfloat16):
    drawn = deviation * jax.random.normal(key, extent, jnp.float32)
    if pieces:
        drawn = drawn * block_levels(key, extent, pieces, -0.22, 0.18)
    return jnp.clip(drawn, -reach, reach).astype(kind)


def setup_inputs(seed: int = 0) -> dict:
    keys = jax.random.split(jax.random.key(seed), 8)
    return {
        "solves": noise(keys[0], (NRHS, ALL_ROWS), 1.0, 6.0, ((0, 4), (1, 128)), jnp.float32),
        "factor3": draw_factor3(jax.random.fold_in(keys[7], 71), 0),
        "factor2": draw_factor2(jax.random.fold_in(keys[7], 71), 0),
        "factor1": draw_factor1(jax.random.fold_in(keys[7], 71), 0),
        "basis3": draw_basis3(jax.random.fold_in(keys[7], 71), 0),
        "basis2": draw_basis2(jax.random.fold_in(keys[7], 71), 0),
        "basis1": draw_basis1(jax.random.fold_in(keys[7], 71), 0),
    }


highest = lax.Precision.HIGHEST

def merge_level(columns, factor, basis_matrix, child_rows):
    node_count = columns.shape[1] // (2 * child_rows)
    rank_width = factor.shape[0]
    blocks = columns.reshape(columns.shape[0], node_count, 2, child_rows)
    factor_blocks = factor.reshape(rank_width, node_count, 2, child_rows)
    basis_blocks = basis_matrix.reshape(rank_width, node_count, 2, child_rows)
    coupling = jnp.einsum('rpcs,qpcs->pcrq', basis_blocks, factor_blocks, precision=highest)
    projected = jnp.einsum('rpcs,kpcs->pcrk', basis_blocks, blocks, precision=highest)
    identity = jnp.broadcast_to(jnp.eye(rank_width, dtype=jnp.float32), (node_count, rank_width, rank_width))
    top_rows = jnp.concatenate([identity, coupling[:, 1]], 2)
    bottom_rows = jnp.concatenate([coupling[:, 0], identity], 2)
    capacity = jnp.concatenate([top_rows, bottom_rows], 1)
    right_side = jnp.concatenate([projected[:, 1], projected[:, 0]], 1)
    solved = jnp.linalg.solve(capacity, right_side)
    halves = solved.reshape(node_count, 2, rank_width, solved.shape[-1])
    update = jnp.einsum('pcrk,rpcs->kpcs', halves, factor_blocks, precision=highest)
    return (blocks - update).reshape(columns.shape)

def reference(solves, factor3, factor2, factor1, basis3, basis2, basis1):
    stacked = jnp.concatenate([solves, factor2, factor1], 0)
    stacked = merge_level(stacked, factor3, basis3, LEAF_ROWS)
    level_two = stacked[NRHS:NRHS + RANK]
    stacked = jnp.concatenate([stacked[:NRHS], stacked[NRHS + RANK:]], 0)
    stacked = merge_level(stacked, level_two, basis2, 2 * LEAF_ROWS)
    return merge_level(stacked[:NRHS], stacked[NRHS:], basis1, 4 * LEAF_ROWS)
```

```python
import functools

import jax
import jax.numpy as jnp
import numpy as np
from jax import lax
from jax.experimental import pallas as pl
from jax.experimental.pallas import tpu as pltpu
from jax.sharding import Mesh, PartitionSpec as P

RANK = 64
LOCAL = 16
ROWS = 4096
HALF = ROWS // 2
CHUNK = 1024
MESSAGE = 160
LIMIT = 48 * 1024 * 1024

LEAF = ("yl", "x", "core")
SLAB = ("yh", "zl", "zh")
BLOCKS = ("zl", "yh", "yl", "x", "core")
NEAR = [(0, 1), (1, 0), (2, 3), (3, 2)]
FAR = [(0, 3), (3, 0), (1, 2), (2, 1)]

bf16 = jnp.bfloat16
f32 = jnp.float32


def split(values):
    high = values.astype(bf16)
    return high, (values - high.astype(f32)).astype(bf16)


def dot(left, right):
    return jnp.dot(left, right, preferred_element_type=f32)


def exact(left, right):
    return jnp.dot(left, right, precision=lax.Precision.HIGHEST, preferred_element_type=f32)


def products(solves, factor3, factor2, factor1, basis3, basis2, basis1, out, total):
    step = pl.program_id(0)
    dims = (((1,), (1,)), ((), ()))
    stacked = jnp.concatenate([solves[...], factor3[...], factor2[...], factor1[...]], 0)
    high, low = split(stacked)
    both = jnp.concatenate([high, low], 0)

    @pl.when(step == 0)
    def _():
        total[...] = jnp.zeros_like(total)

    for slot, basis in enumerate((basis3, basis2, basis1)):
        top, rest = split(basis[...])
        wide = lax.dot_general(both, top, dims, preferred_element_type=f32)
        thin = lax.dot_general(high, rest, dims, preferred_element_type=f32)
        total[slot] += wide[:RANK] + (wide[RANK:] + thin)

    @pl.when(step == pl.num_programs(0) - 1)
    def _():
        for slot in range(3):
            here = total[slot]
            out[:, 2 * slot, :] = jnp.concatenate([here[0:16], here[32:48]], 1)
            out[:, 2 * slot + 1, :] = jnp.concatenate([here[16:32], here[48:64]], 1)
        out[:, 6, :] = jnp.zeros((16, 128), f32)
        out[:, 7, :] = jnp.zeros((16, 128), f32)


def local_products(*arrays):
    narrow = pl.BlockSpec((LOCAL, CHUNK), lambda i: (0, i))
    wide = pl.BlockSpec((RANK, CHUNK), lambda i: (0, i))
    return pl.pallas_call(
        products,
        grid=(ROWS // CHUNK,),
        in_specs=[narrow] * 4 + [wide] * 3,
        out_specs=pl.BlockSpec((16, 8, 128), lambda i: (0, 0, 0)),
        out_shape=jax.ShapeDtypeStruct((16, 8, 128), f32),
        scratch_shapes=[pltpu.VMEM((3, RANK, RANK), f32)],
        cost_estimate=pl.CostEstimate(
            flops=2 * 3 * 192 * 64 * ROWS, bytes_accessed=ROWS * 256 * 4, transcendentals=0
        ),
    )(*arrays)


def leaf_sum(pieces, out):
    total = pieces[0]
    for index in range(1, 16):
        total = total + pieces[index]
    out[...] = jnp.broadcast_to(total[None], out.shape)


def pack(pieces, out):
    rows = [pieces[:, index, :] for index in range(6)]
    message = jnp.concatenate(
        [
            rows[0],
            rows[1],
            rows[3],
            rows[5],
            rows[2][:16] + rows[2][16:],
            rows[4][:16] + rows[4][16:],
        ],
        0,
    )
    out[...] = jnp.broadcast_to(message[None], out.shape)


def inverses(matrices):
    eye = (
        lax.broadcasted_iota(jnp.int32, (RANK, RANK), 0)
        == lax.broadcasted_iota(jnp.int32, (RANK, RANK), 1)
    ).astype(f32)
    starts = []
    for matrix in matrices:
        size = jnp.abs(matrix)
        by_row = jnp.max(jnp.sum(size, 1, keepdims=True), 0, keepdims=True)
        by_column = jnp.max(jnp.sum(size, 0, keepdims=True), 1, keepdims=True)
        starts.append(matrix.T / by_row / by_column)

    def improve(state):
        count, _, guesses = state
        gaps = [eye - exact(m, g) for m, g in zip(matrices, guesses)]
        worst = gaps[0] * gaps[0]
        for gap in gaps[1:]:
            worst = worst + gap * gap
        better = tuple(g + exact(g, gap) for g, gap in zip(guesses, gaps))
        return count + 1, jnp.sum(worst), better

    def unfinished(state):
        count, error, _ = state
        return (count < 64) & jnp.logical_not(error <= 1e-7)

    state = lax.while_loop(unfinished, improve, (jnp.int32(0), jnp.float32(1.0), tuple(starts)))
    return state[2]


def merge(nodes):
    eye = (
        lax.broadcasted_iota(jnp.int32, (RANK, RANK), 0)
        == lax.broadcasted_iota(jnp.int32, (RANK, RANK), 1)
    ).astype(f32)
    reduced = [eye - exact(kb, ka) for ka, kb, _, _ in nodes]
    sides = [ra - exact(rb, ka) for ka, _, ra, rb in nodes]
    turned = inverses(reduced)
    bottoms = [exact(side, inv) for side, inv in zip(sides, turned)]
    tops = [rb - exact(low, kb) for (_, kb, _, rb), low in zip(nodes, bottoms)]
    return tops, bottoms


def tree(place, sums, near_out, far_out, first, second, third, whole):
    def rows(base, entry):
        return jnp.concatenate(
            [sums[pl.ds(base + entry * 4 + zh, 16, stride=MESSAGE), :] for zh in range(4)], 0
        )

    def left(values):
        return values[:, :RANK]

    def right(values):
        return values[:, RANK:]

    nodes = []
    couple = []
    carry2 = []
    carry1 = []
    for zl in range(4):
        xa, xb = rows(0, zl), rows(0, 4 + zl)
        fa, fb = rows(32, zl), rows(32, 4 + zl)
        nodes.append(
            (
                left(fa),
                left(fb),
                jnp.concatenate([left(xa), right(xa), right(fa)], 0),
                jnp.concatenate([left(xb), right(xb), right(fb)], 0),
            )
        )
        ga, gb = rows(64, zl), rows(64, 4 + zl)
        ha, hb = rows(96, zl), rows(96, 4 + zl)
        x2, x1 = rows(128, zl), rows(144, zl)
        couple.append(
            (
                jnp.concatenate([left(ga), left(ha)], 1),
                jnp.concatenate([left(gb), left(hb)], 1),
            )
        )
        carry2.append(jnp.concatenate([left(x2), right(x2), right(ga) + right(gb)], 0))
        carry1.append(jnp.concatenate([left(x1), right(x1), right(ha) + right(hb)], 0))
    tops, bottoms = merge(nodes)
    two = []
    one = []
    for zl in range(4):
        third[2 * zl] = tops[zl]
        third[2 * zl + 1] = bottoms[zl]
        update = exact(tops[zl], couple[zl][0]) + exact(bottoms[zl], couple[zl][1])
        two.append(carry2[zl] - left(update))
        one.append(carry1[zl] - right(update))

    def keep(values):
        return jnp.concatenate([values[:RANK], values[2 * RANK :]], 0)

    nodes = [
        (
            two[2 * m][RANK : 2 * RANK],
            two[2 * m + 1][RANK : 2 * RANK],
            keep(two[2 * m]),
            keep(two[2 * m + 1]),
        )
        for m in range(2)
    ]
    tops, bottoms = merge(nodes)
    last = []
    for m in range(2):
        second[2 * m] = tops[m]
        second[2 * m + 1] = bottoms[m]
        last.append(
            keep(one[2 * m])
            + keep(one[2 * m + 1])
            - exact(tops[m], one[2 * m][RANK : 2 * RANK])
            - exact(bottoms[m], one[2 * m + 1][RANK : 2 * RANK])
        )
    tops, bottoms = merge([(last[0][RANK:], last[1][RANK:], last[0][:RANK], last[1][:RANK])])
    first[0] = tops[0]
    first[1] = bottoms[0]

    zl, yh, zh = place[0], place[1], place[2]
    near = place[3]
    far = place[4]
    c3 = third[2 * zl + yh]
    c2 = second[zl]
    d1 = first[zl // 2]
    d2 = c2[:RANK] - exact(d1, c2[RANK:])
    d3 = c3[:RANK] - exact(d2, c3[RANK : 2 * RANK]) - exact(d1, c3[2 * RANK :])
    whole[...] = jnp.concatenate([d3, d2, d1], 1)

    def chosen(partner, target):
        picked = jnp.concatenate(
            [whole[pl.ds(zh * 16, 16), :], whole[pl.ds(target * 16, 16), :]], 0
        )
        source = lax.broadcasted_iota(jnp.int32, (192, 96), 0)
        column = lax.broadcasted_iota(jnp.int32, (192, 96), 1)
        owner = jnp.where(column < 48, zh, partner)
        inner = jnp.where(column < 48, column, column - 48)
        wanted = (inner // 16) * RANK + owner * 16 + inner % 16
        return -exact(picked, (source == wanted).astype(f32))

    near_out[...] = chosen(near, far)
    far_out[...] = chosen(far, near)


def apply_rows(coefficient, own, other):
    high, low = split(coefficient)
    both = jnp.concatenate([high, low], 0)
    factor = jnp.concatenate([own, other], 0)
    top, rest = split(factor)
    wide = dot(both, top)
    return wide[:16] + (wide[16:] + dot(high, rest))


def outgoing(near_c, far_c, own_a, own_b, got_a, got_b, out_a, out_b):
    out_a[...] = apply_rows(near_c[16:], own_a[...], got_a[...])
    out_b[...] = apply_rows(far_c[16:], own_b[...], got_b[...])


def staying(near_c, far_c, own_a, own_b, got_a, got_b, solves, out):
    out[:, :HALF] = solves[:, :HALF] + apply_rows(near_c[:16], own_a[...], got_a[...])
    out[:, HALF:] = solves[:, HALF:] + apply_rows(far_c[:16], own_b[...], got_b[...])


def call(kernel, shapes, *arrays, scratch=(), **kwargs):
    return pl.pallas_call(
        kernel,
        out_shape=shapes,
        scratch_shapes=list(scratch),
        compiler_params=pltpu.CompilerParams(vmem_limit_bytes=LIMIT),
        **kwargs,
    )(*arrays)


def shape(*dims):
    return jax.ShapeDtypeStruct(dims, f32)


def on_device(solves, factor3, factor2, factor1, basis3, basis2, basis1):
    zh = lax.axis_index("zh")
    own_a = jnp.concatenate([factor3[:, :HALF], factor2[:, :HALF], factor1[:, :HALF]], 0)
    own_b = jnp.concatenate([factor3[:, HALF:], factor2[:, HALF:], factor1[:, HALF:]], 0)
    got_a = lax.ppermute(own_a, "zh", NEAR)
    got_b = lax.ppermute(own_b, "zh", FAR)
    slots = local_products(solves, factor3, factor2, factor1, basis3, basis2, basis1)
    pieces = lax.all_to_all(slots, LEAF, 0, 0, tiled=True)
    copies = call(leaf_sum, shape(32, 8, 128), pieces)
    slabs = lax.all_to_all(copies, SLAB, 0, 0, tiled=True)
    message = call(pack, shape(16, MESSAGE, 128), slabs)
    sums = lax.all_to_all(message, LEAF, 0, 0, tiled=True).reshape(16 * MESSAGE, 128)
    place = jnp.stack(
        [lax.axis_index("zl"), lax.axis_index("yh"), zh, zh ^ 1, 3 - zh]
    ).astype(jnp.int32)
    vmem = pl.BlockSpec(memory_space=pltpu.VMEM)
    near_c, far_c = call(
        tree,
        (shape(32, 96), shape(32, 96)),
        place,
        sums,
        in_specs=[pl.BlockSpec(memory_space=pltpu.SMEM), vmem],
        out_specs=(vmem, vmem),
        scratch=[
            pltpu.VMEM((2, 64, 64), f32),
            pltpu.VMEM((4, 128, 64), f32),
            pltpu.VMEM((8, 192, 64), f32),
            pltpu.VMEM((64, 192), f32),
        ],
    )
    blocks = (near_c, far_c, own_a, own_b, got_a, got_b)
    cost = pl.CostEstimate(flops=2 * 3 * 96 * 16 * ROWS, bytes_accessed=96 * ROWS * 4, transcendentals=0)
    send_a, send_b = call(outgoing, (shape(16, HALF), shape(16, HALF)), *blocks, cost_estimate=cost)
    came_a = lax.ppermute(send_a, "zh", FAR)
    came_b = lax.ppermute(send_b, "zh", NEAR)
    kept = call(staying, shape(16, ROWS), *blocks, solves, cost_estimate=cost)
    return kept + jnp.concatenate([came_a, came_b], 1)


def solution(mesh):
    fine = Mesh(
        mesh.devices.reshape(4, 2, 2, 4, 2, 4), ("zl", "yh", "yl", "x", "core", "zh")
    )
    split_both = P("zh", BLOCKS)
    split_rows = P(None, BLOCKS)
    return jax.shard_map(
        on_device,
        mesh=fine,
        in_specs=(split_both,) * 4 + (split_rows,) * 3,
        out_specs=split_both,
        check_vma=False,
    )
```

```python
import functools

import jax
import jax.numpy as jnp
import numpy as np
from jax import lax
from jax.experimental import pallas as pl
from jax.experimental.pallas import tpu as pltpu
from jax.sharding import Mesh, PartitionSpec as P

RANK = 64
LOCAL = 16
ROWS = 4096
CHUNK = 1024
MESSAGE = 144
LIMIT = 48 * 1024 * 1024

LEAF = ("yl", "x", "core")
SLAB = ("yh", "zl", "zh")
BLOCKS = ("zl", "yh", "yl", "x", "core")
PAIRS = ("core", "zh")
SWAP = [(0, 1), (1, 0), (2, 3), (3, 2), (4, 7), (7, 4), (5, 6), (6, 5)]
RETURN = [(0, 3), (3, 0), (1, 2), (2, 1), (4, 5), (5, 4), (6, 7), (7, 6)]

bf16 = jnp.bfloat16
f32 = jnp.float32


def split(values):
    high = values.astype(bf16)
    return high, (values - high.astype(f32)).astype(bf16)


def dot(left, right):
    return jnp.dot(left, right, preferred_element_type=f32)


def exact(left, right):
    return full(left, right)


FREE = pl.CostEstimate(flops=0, bytes_accessed=0, transcendentals=0)


def full(left, right):
    count = left.shape[0]
    top, middle = split(left)
    low = (left - top.astype(f32) - middle.astype(f32)).astype(bf16)
    right_top, right_middle = split(right)
    right_low = (right - right_top.astype(f32) - right_middle.astype(f32)).astype(bf16)
    first = dot(jnp.concatenate([top, middle, low], 0), right_top)
    second = dot(jnp.concatenate([top, middle], 0), right_middle)
    third = dot(top, right_low)
    small = first[2 * count :] + second[count:] + third
    return first[:count] + (first[count : 2 * count] + second[:count] + small)


def products(
    solves, factor3, factor2, factor1, basis3, basis2, basis1, out, own, total3, total21
):
    step = pl.program_id(0)
    dims = (((1,), (1,)), ((), ()))
    factors = jnp.concatenate([factor2[...], factor1[...]], 0)
    own[...] = factors
    high, low = split(jnp.concatenate([solves[...], factor3[...], factors], 0))
    both = jnp.concatenate([high, low], 0)

    @pl.when(step == 0)
    def _():
        total3[...] = jnp.zeros_like(total3)
        total21[...] = jnp.zeros_like(total21)

    for total, basis in (
        (total3, basis3[...]),
        (total21, jnp.concatenate([basis2[...], basis1[...]], 0)),
    ):
        top, rest = split(basis)
        wide = lax.dot_general(both, top, dims, preferred_element_type=f32)
        thin = lax.dot_general(high, rest, dims, preferred_element_type=f32)
        total[...] += wide[:RANK] + (wide[RANK:] + thin)

    @pl.when(step == pl.num_programs(0) - 1)
    def _():
        deep = total3[...]
        out[:, 0, :] = jnp.concatenate([deep[0:16], deep[32:48]], 1)
        out[:, 1, :] = jnp.concatenate([deep[16:32], deep[48:64]], 1)
        out[:, 2, :] = total21[16:32, :]
        out[:, 3, :] = total21[0:16, :]
        out[:, 4, :] = total21[32:48, :]
        out[:, 5, :] = total21[48:64, :]
        out[:, 6, :] = jnp.zeros((16, 128), f32)
        out[:, 7, :] = jnp.zeros((16, 128), f32)


def local_products(*arrays):
    narrow = pl.BlockSpec((LOCAL, CHUNK), lambda i: (0, i))
    wide = pl.BlockSpec((RANK, CHUNK), lambda i: (0, i))
    return pl.pallas_call(
        products,
        grid=(ROWS // CHUNK,),
        in_specs=[narrow] * 4 + [wide] * 3,
        out_specs=(
            pl.BlockSpec((16, 8, 128), lambda i: (0, 0, 0)),
            pl.BlockSpec((2 * LOCAL, CHUNK), lambda i: (0, i)),
        ),
        out_shape=(shape(16, 8, 128), shape(2 * LOCAL, ROWS)),
        scratch_shapes=[pltpu.VMEM((RANK, RANK), f32), pltpu.VMEM((RANK, 2 * RANK), f32)],
        cost_estimate=FREE,
    )(*arrays)


def leaf_sum(pieces, out):
    total = pieces[0]
    for index in range(1, 16):
        total = total + pieces[index]
    out[...] = jnp.broadcast_to(total[None], out.shape)


def pack(pieces, out):
    rows = [pieces[:, index, :] for index in range(6)]
    paired = [rows[index][:16] + rows[index][16:] for index in (3, 4, 5)]
    message = jnp.concatenate(rows[:3] + paired, 0)
    out[...] = jnp.broadcast_to(message[None], out.shape)


def identity():
    return (
        lax.broadcasted_iota(jnp.int32, (RANK, RANK), 0)
        == lax.broadcasted_iota(jnp.int32, (RANK, RANK), 1)
    ).astype(f32)


def squares(matrices):
    total = matrices[0] * matrices[0]
    for matrix in matrices[1:]:
        total = total + matrix * matrix
    return jnp.sum(total)


def inverses(crossed, scratch):
    eye = identity()
    size = squares(crossed)
    close = size < 0.8

    @pl.when(close)
    def _():
        def improve(state):
            powers, guesses, _ = state
            both = [full(jnp.concatenate([e, g], 0), e) for g, e in zip(guesses, powers)]
            better = tuple(g + b[RANK:] for g, b in zip(guesses, both))
            return tuple(b[:RANK] for b in both), better, squares(powers)

        def unfinished(state):
            return state[2] > 1e-8

        first = tuple(full(e, e) for e in crossed)
        state = lax.while_loop(
            unfinished, improve, (first, tuple(eye + e for e in crossed), size)
        )
        for index, guess in enumerate(state[1]):
            scratch[index] = guess

    @pl.when(jnp.logical_not(close))
    def _():
        matrices = [eye - e for e in crossed]
        starts = []
        for matrix in matrices:
            level = jnp.abs(matrix)
            by_row = jnp.max(jnp.sum(level, 1, keepdims=True), 0, keepdims=True)
            by_column = jnp.max(jnp.sum(level, 0, keepdims=True), 1, keepdims=True)
            starts.append(matrix.T / by_row / by_column)

        def improve(state):
            count, _, guesses = state
            gaps = [eye - exact(m, g) for m, g in zip(matrices, guesses)]
            better = tuple(g + exact(g, gap) for g, gap in zip(guesses, gaps))
            return count + 1, squares(gaps), better

        def unfinished(state):
            count, error, _ = state
            return (count < 64) & jnp.logical_not(error <= 1e-7)

        state = lax.while_loop(
            unfinished, improve, (jnp.int32(0), jnp.float32(1.0), tuple(starts))
        )
        for index, guess in enumerate(state[2]):
            scratch[index] = guess


def merge(nodes, scratch):
    crossed = [exact(kb, ka) for ka, kb, _, _ in nodes]
    sides = [ra - exact(rb, ka) for ka, _, ra, rb in nodes]
    inverses(crossed, scratch)
    bottoms = [exact(side, scratch[index]) for index, side in enumerate(sides)]
    tops = [rb - exact(low, kb) for (_, kb, _, rb), low in zip(nodes, bottoms)]
    return tops, bottoms


def tree(place, sums, out, first, second, third, whole, solved):
    def rows(base, entry):
        return jnp.concatenate(
            [sums[pl.ds(base + entry * 4 + zh, 16, stride=MESSAGE), :] for zh in range(4)], 0
        )

    def left(values):
        return values[:, :RANK]

    def right(values):
        return values[:, RANK:]

    nodes = []
    couple = []
    carry = []
    for zl in range(4):
        xa, xb = rows(0, zl), rows(0, 4 + zl)
        fa, fb = rows(32, zl), rows(32, 4 + zl)
        nodes.append(
            (
                left(fa),
                left(fb),
                jnp.concatenate([left(xa), right(xa), right(fa)], 0),
                jnp.concatenate([left(xb), right(xb), right(fb)], 0),
            )
        )
        couple.append((rows(64, zl), rows(64, 4 + zl)))
        carry.append(jnp.concatenate([rows(96, zl), rows(112, zl), rows(128, zl)], 0))
    tops, bottoms = merge(nodes, solved)
    two = []
    one = []
    for zl in range(4):
        third[2 * zl] = tops[zl]
        third[2 * zl + 1] = bottoms[zl]
        update = exact(tops[zl], couple[zl][0]) + exact(bottoms[zl], couple[zl][1])
        carried = carry[zl] - update
        two.append(left(carried))
        one.append(right(carried))

    def keep(values):
        return jnp.concatenate([values[:RANK], values[2 * RANK :]], 0)

    nodes = [
        (
            two[2 * m][RANK : 2 * RANK],
            two[2 * m + 1][RANK : 2 * RANK],
            keep(two[2 * m]),
            keep(two[2 * m + 1]),
        )
        for m in range(2)
    ]
    tops, bottoms = merge(nodes, solved)
    last = []
    for m in range(2):
        second[2 * m] = tops[m]
        second[2 * m + 1] = bottoms[m]
        last.append(
            keep(one[2 * m])
            + keep(one[2 * m + 1])
            - exact(tops[m], one[2 * m][RANK : 2 * RANK])
            - exact(bottoms[m], one[2 * m + 1][RANK : 2 * RANK])
        )
    tops, bottoms = merge([(last[0][RANK:], last[1][RANK:], last[0][:RANK], last[1][:RANK])], solved)
    first[0] = tops[0]
    first[1] = bottoms[0]

    zl, yh, zh = place[0], place[1], place[2]
    partner = place[3]
    target = place[4]
    c3 = third[2 * zl + yh]
    c2 = second[zl]
    d1 = first[zl // 2]
    d2 = c2[:RANK] - exact(d1, c2[RANK:])
    d3 = c3[:RANK] - exact(d2, c3[RANK : 2 * RANK]) - exact(d1, c3[2 * RANK :])
    whole[...] = jnp.concatenate([d3, d2, d1], 1)

    picked = jnp.concatenate(
        [whole[pl.ds(zh * 16, 16), :], whole[pl.ds(target * 16, 16), :]], 0
    )
    source = lax.broadcasted_iota(jnp.int32, (192, 128), 0)
    column = lax.broadcasted_iota(jnp.int32, (192, 128), 1)
    owner = jnp.where(column < 48, zh, partner)
    inner = jnp.where(column < 48, column, column - 48)
    wanted = (inner // 16) * RANK + owner * 16 + inner % 16
    out[...] = -exact(picked, ((source == wanted) & (column < 96)).astype(f32))


def apply_rows(coefficient, *factors):
    high, low = split(coefficient)
    both = jnp.concatenate([high, low], 0)
    top, rest = split(jnp.concatenate([factor[...] for factor in factors], 0))
    wide = dot(both, top)
    return wide[:16] + (wide[16:] + dot(high, rest))


def outgoing(weights, own3, own, got3, got, out):
    out[...] = apply_rows(weights[16:32, :96], own3, own, got3, got)


def staying(weights, own3, own, got3, got, solves, out):
    out[...] = solves[...] + apply_rows(weights[0:16, :96], own3, own, got3, got)


def call(kernel, shapes, *arrays, scratch=(), **kwargs):
    return pl.pallas_call(
        kernel,
        out_shape=shapes,
        scratch_shapes=list(scratch),
        compiler_params=pltpu.CompilerParams(vmem_limit_bytes=LIMIT),
        cost_estimate=FREE,
        **kwargs,
    )(*arrays)


def shape(*dims):
    return jax.ShapeDtypeStruct(dims, f32)


def on_device(solves, factor3, factor2, factor1, basis3, basis2, basis1):
    zh = lax.axis_index("zh")
    core = lax.axis_index("core")
    near, far = zh ^ 1, 3 - zh
    place = jnp.stack(
        [
            lax.axis_index("zl"),
            lax.axis_index("yh"),
            zh,
            jnp.where(core == 0, near, far),
            jnp.where(core == 0, far, near),
        ]
    ).astype(jnp.int32)
    got3 = lax.ppermute(factor3, PAIRS, SWAP)
    slots, own = local_products(solves, factor3, factor2, factor1, basis3, basis2, basis1)
    slots, place = lax.optimization_barrier((slots, place))
    got = lax.ppermute(own, PAIRS, SWAP)
    pieces = lax.all_to_all(slots, LEAF, 0, 0, tiled=True)
    vmem = pl.BlockSpec(memory_space=pltpu.VMEM)

    copies = call(leaf_sum, shape(32, 8, 128), pieces)
    copies, got3 = lax.optimization_barrier((copies, got3))
    slabs = lax.all_to_all(copies, SLAB, 0, 0, tiled=True)
    message = call(pack, shape(16, MESSAGE, 128), slabs)
    sums = lax.all_to_all(message, LEAF, 0, 0, tiled=True).reshape(16 * MESSAGE, 128)
    coefficients = call(
        tree,
        shape(32, 128),
        place,
        sums,
        in_specs=[pl.BlockSpec(memory_space=pltpu.SMEM), vmem],
        out_specs=vmem,
        scratch=[
            pltpu.VMEM((2, 64, 64), f32),
            pltpu.VMEM((4, 128, 64), f32),
            pltpu.VMEM((8, 192, 64), f32),
            pltpu.VMEM((64, 192), f32),
            pltpu.VMEM((4, 64, 64), f32),
        ],
    )
    sent = call(outgoing, shape(16, ROWS), coefficients, factor3, own, got3, got)
    came = lax.ppermute(sent, PAIRS, RETURN)
    return call(staying, shape(16, ROWS), coefficients, factor3, own, got3, got, solves) + came


def solution(mesh):
    fine = Mesh(
        mesh.devices.reshape(4, 2, 2, 4, 2, 4), ("zl", "yh", "yl", "x", "core", "zh")
    )
    split_both = P("zh", BLOCKS)
    split_rows = P(None, BLOCKS)
    return jax.shard_map(
        on_device,
        mesh=fine,
        in_specs=(split_both,) * 4 + (split_rows,) * 3,
        out_specs=split_both,
        check_vma=False,
    )
```

```python
import functools

import jax
import jax.numpy as jnp
import numpy as np
from jax import lax
from jax.experimental import pallas as pl
from jax.experimental.pallas import tpu as pltpu
from jax.sharding import Mesh, PartitionSpec as P

RANK = 64
LOCAL = 16
ROWS = 4096
CHUNK = 2048
MESSAGE = 144
LIMIT = 48 * 1024 * 1024

LEAF = ("yl", "x", "core")
SLAB = ("yh", "zl", "zh")
BLOCKS = ("zl", "yh", "yl", "x", "core")
PAIRS = ("core", "zh")
SWAP = [(0, 1), (1, 0), (2, 3), (3, 2), (4, 7), (7, 4), (5, 6), (6, 5)]
RETURN = [(0, 3), (3, 0), (1, 2), (2, 1), (4, 5), (5, 4), (6, 7), (7, 6)]

bf16 = jnp.bfloat16
f32 = jnp.float32


def split(values):
    high = values.astype(bf16)
    return high, (values - high.astype(f32)).astype(bf16)


def dot(left, right):
    return jnp.dot(left, right, preferred_element_type=f32)


def exact(left, right):
    return full(left, right)


FREE = pl.CostEstimate(flops=0, bytes_accessed=0, transcendentals=0)


def full(left, right):
    count = left.shape[0]
    top, middle = split(left)
    low = (left - top.astype(f32) - middle.astype(f32)).astype(bf16)
    right_top, right_middle = split(right)
    right_low = (right - right_top.astype(f32) - right_middle.astype(f32)).astype(bf16)
    first = dot(jnp.concatenate([top, middle, low], 0), right_top)
    second = dot(jnp.concatenate([top, middle], 0), right_middle)
    third = dot(top, right_low)
    small = first[2 * count :] + second[count:] + third
    return first[:count] + (first[count : 2 * count] + second[:count] + small)


def products(
    solves, factor3, factor2, factor1, basis3, basis2, basis1, out, own, total3, total21
):
    step = pl.program_id(0)
    dims = (((1,), (1,)), ((), ()))
    factors = jnp.concatenate([factor2[...], factor1[...]], 0)
    own[...] = factors
    high, low = split(jnp.concatenate([solves[...], factor3[...], factors], 0))
    both = jnp.concatenate([high, low], 0)

    @pl.when(step == 0)
    def _():
        total3[...] = jnp.zeros_like(total3)
        total21[...] = jnp.zeros_like(total21)

    for total, basis in (
        (total3, basis3[...]),
        (total21, jnp.concatenate([basis2[...], basis1[...]], 0)),
    ):
        top, rest = split(basis)
        wide = lax.dot_general(both, top, dims, preferred_element_type=f32)
        thin = lax.dot_general(high, rest, dims, preferred_element_type=f32)
        total[...] += wide[:RANK] + (wide[RANK:] + thin)

    @pl.when(step == pl.num_programs(0) - 1)
    def _():
        deep = total3[...]
        out[:, 0, :] = jnp.concatenate([deep[0:16], deep[32:48]], 1)
        out[:, 1, :] = jnp.concatenate([deep[16:32], deep[48:64]], 1)
        out[:, 2, :] = total21[16:32, :]
        out[:, 3, :] = total21[0:16, :]
        out[:, 4, :] = total21[32:48, :]
        out[:, 5, :] = total21[48:64, :]
        out[:, 6, :] = jnp.zeros((16, 128), f32)
        out[:, 7, :] = jnp.zeros((16, 128), f32)


def local_products(*arrays):
    narrow = pl.BlockSpec((LOCAL, CHUNK), lambda i: (0, i))
    wide = pl.BlockSpec((RANK, CHUNK), lambda i: (0, i))
    return pl.pallas_call(
        products,
        grid=(ROWS // CHUNK,),
        in_specs=[narrow] * 4 + [wide] * 3,
        out_specs=(
            pl.BlockSpec((16, 8, 128), lambda i: (0, 0, 0)),
            pl.BlockSpec((2 * LOCAL, CHUNK), lambda i: (0, i)),
        ),
        out_shape=(shape(16, 8, 128), shape(2 * LOCAL, ROWS)),
        scratch_shapes=[pltpu.VMEM((RANK, RANK), f32), pltpu.VMEM((RANK, 2 * RANK), f32)],
        cost_estimate=FREE,
    )(*arrays)


def leaf_sum(pieces, out):
    total = pieces[0]
    for index in range(1, 16):
        total = total + pieces[index]
    out[...] = jnp.broadcast_to(total[None], out.shape)


def pack(pieces, out):
    rows = [pieces[:, index, :] for index in range(6)]
    paired = [rows[index][:16] + rows[index][16:] for index in (3, 4, 5)]
    message = jnp.concatenate(rows[:3] + paired, 0)
    out[...] = jnp.broadcast_to(message[None], out.shape)


def identity():
    return (
        lax.broadcasted_iota(jnp.int32, (RANK, RANK), 0)
        == lax.broadcasted_iota(jnp.int32, (RANK, RANK), 1)
    ).astype(f32)


def squares(matrices):
    total = matrices[0] * matrices[0]
    for matrix in matrices[1:]:
        total = total + matrix * matrix
    return jnp.sum(total)


def inverses(crossed, scratch):
    eye = identity()
    seconds = [full(e, e) for e in crossed]
    close = squares(seconds) < 0.8

    @pl.when(close)
    def _():
        def improve(state):
            powers, guesses, _ = state
            both = [full(jnp.concatenate([p, g], 0), p) for g, p in zip(guesses, powers)]
            better = tuple(g + b[RANK:] for g, b in zip(guesses, both))
            higher = tuple(b[:RANK] for b in both)
            return higher, better, squares(powers)

        def unfinished(state):
            return state[2] > 1e-7

        state = lax.while_loop(
            unfinished,
            improve,
            (tuple(seconds), tuple(eye + e for e in crossed), jnp.float32(1.0)),
        )
        for index, guess in enumerate(state[1]):
            scratch[index] = guess

    @pl.when(jnp.logical_not(close))
    def _():
        matrices = [eye - e for e in crossed]
        starts = []
        for matrix in matrices:
            level = jnp.abs(matrix)
            by_row = jnp.max(jnp.sum(level, 1, keepdims=True), 0, keepdims=True)
            by_column = jnp.max(jnp.sum(level, 0, keepdims=True), 1, keepdims=True)
            starts.append(matrix.T / by_row / by_column)

        def improve(state):
            count, _, guesses = state
            gaps = [eye - exact(m, g) for m, g in zip(matrices, guesses)]
            better = tuple(g + exact(g, gap) for g, gap in zip(guesses, gaps))
            return count + 1, squares(gaps), better

        def unfinished(state):
            count, error, _ = state
            return (count < 64) & jnp.logical_not(error <= 1e-7)

        state = lax.while_loop(
            unfinished, improve, (jnp.int32(0), jnp.float32(1.0), tuple(starts))
        )
        for index, guess in enumerate(state[2]):
            scratch[index] = guess


def merge(nodes, scratch):
    crossed = [exact(kb, ka) for ka, kb, _, _ in nodes]
    sides = [ra - exact(rb, ka) for ka, _, ra, rb in nodes]
    inverses(crossed, scratch)
    bottoms = [exact(side, scratch[index]) for index, side in enumerate(sides)]
    tops = [rb - exact(low, kb) for (_, kb, _, rb), low in zip(nodes, bottoms)]
    return tops, bottoms


def tree(place, sums, out, first, second, third, whole, solved):
    def rows(base, entry):
        return jnp.concatenate(
            [sums[pl.ds(base + entry * 4 + zh, 16, stride=MESSAGE), :] for zh in range(4)], 0
        )

    def left(values):
        return values[:, :RANK]

    def right(values):
        return values[:, RANK:]

    nodes = []
    couple = []
    carry = []
    for zl in range(4):
        xa, xb = rows(0, zl), rows(0, 4 + zl)
        fa, fb = rows(32, zl), rows(32, 4 + zl)
        nodes.append(
            (
                left(fa),
                left(fb),
                jnp.concatenate([left(xa), right(xa), right(fa)], 0),
                jnp.concatenate([left(xb), right(xb), right(fb)], 0),
            )
        )
        couple.append((rows(64, zl), rows(64, 4 + zl)))
        carry.append(jnp.concatenate([rows(96, zl), rows(112, zl), rows(128, zl)], 0))
    tops, bottoms = merge(nodes, solved)
    two = []
    one = []
    for zl in range(4):
        third[2 * zl] = tops[zl]
        third[2 * zl + 1] = bottoms[zl]
        update = exact(tops[zl], couple[zl][0]) + exact(bottoms[zl], couple[zl][1])
        carried = carry[zl] - update
        two.append(left(carried))
        one.append(right(carried))

    def keep(values):
        return jnp.concatenate([values[:RANK], values[2 * RANK :]], 0)

    nodes = [
        (
            two[2 * m][RANK : 2 * RANK],
            two[2 * m + 1][RANK : 2 * RANK],
            keep(two[2 * m]),
            keep(two[2 * m + 1]),
        )
        for m in range(2)
    ]
    tops, bottoms = merge(nodes, solved)
    last = []
    for m in range(2):
        second[2 * m] = tops[m]
        second[2 * m + 1] = bottoms[m]
        last.append(
            keep(one[2 * m])
            + keep(one[2 * m + 1])
            - exact(tops[m], one[2 * m][RANK : 2 * RANK])
            - exact(bottoms[m], one[2 * m + 1][RANK : 2 * RANK])
        )
    tops, bottoms = merge([(last[0][RANK:], last[1][RANK:], last[0][:RANK], last[1][:RANK])], solved)
    first[0] = tops[0]
    first[1] = bottoms[0]

    zl, yh, zh = place[0], place[1], place[2]
    partner = place[3]
    target = place[4]
    c3 = third[2 * zl + yh]
    c2 = second[zl]
    d1 = first[zl // 2]
    d2 = c2[:RANK] - exact(d1, c2[RANK:])
    d3 = c3[:RANK] - exact(d2, c3[RANK : 2 * RANK]) - exact(d1, c3[2 * RANK :])
    whole[...] = jnp.concatenate([d3, d2, d1], 1)

    picked = jnp.concatenate(
        [whole[pl.ds(zh * 16, 16), :], whole[pl.ds(target * 16, 16), :]], 0
    )
    source = lax.broadcasted_iota(jnp.int32, (192, 128), 0)
    column = lax.broadcasted_iota(jnp.int32, (192, 128), 1)
    owner = jnp.where(column < 48, zh, partner)
    inner = jnp.where(column < 48, column, column - 48)
    wanted = (inner // 16) * RANK + owner * 16 + inner % 16
    out[...] = -exact(picked, ((source == wanted) & (column < 96)).astype(f32))


def apply_rows(coefficient, *factors):
    high, low = split(coefficient)
    both = jnp.concatenate([high, low], 0)
    top, rest = split(jnp.concatenate([factor[...] for factor in factors], 0))
    wide = dot(both, top)
    return wide[:16] + (wide[16:] + dot(high, rest))


def outgoing(weights, own3, own, got3, got, out):
    out[...] = apply_rows(weights[16:32, :96], own3, own, got3, got)


def staying(weights, own3, own, got3, got, solves, out):
    out[...] = solves[...] + apply_rows(weights[0:16, :96], own3, own, got3, got)


def call(kernel, shapes, *arrays, scratch=(), **kwargs):
    return pl.pallas_call(
        kernel,
        out_shape=shapes,
        scratch_shapes=list(scratch),
        compiler_params=pltpu.CompilerParams(vmem_limit_bytes=LIMIT),
        cost_estimate=FREE,
        **kwargs,
    )(*arrays)


def shape(*dims):
    return jax.ShapeDtypeStruct(dims, f32)


def on_device(solves, factor3, factor2, factor1, basis3, basis2, basis1):
    zh = lax.axis_index("zh")
    core = lax.axis_index("core")
    near, far = zh ^ 1, 3 - zh
    place = jnp.stack(
        [
            lax.axis_index("zl"),
            lax.axis_index("yh"),
            zh,
            jnp.where(core == 0, near, far),
            jnp.where(core == 0, far, near),
        ]
    ).astype(jnp.int32)
    got3 = lax.ppermute(factor3, PAIRS, SWAP)
    slots, own = local_products(solves, factor3, factor2, factor1, basis3, basis2, basis1)
    slots, place = lax.optimization_barrier((slots, place))
    got = lax.ppermute(own, PAIRS, SWAP)
    pieces = lax.all_to_all(slots, LEAF, 0, 0, tiled=True)
    vmem = pl.BlockSpec(memory_space=pltpu.VMEM)

    copies = call(leaf_sum, shape(32, 8, 128), pieces)
    copies, got3 = lax.optimization_barrier((copies, got3))
    slabs = lax.all_to_all(copies, SLAB, 0, 0, tiled=True)
    message = call(pack, shape(16, MESSAGE, 128), slabs)
    sums = lax.all_to_all(message, LEAF, 0, 0, tiled=True).reshape(16 * MESSAGE, 128)
    coefficients = call(
        tree,
        shape(32, 128),
        place,
        sums,
        in_specs=[pl.BlockSpec(memory_space=pltpu.SMEM), vmem],
        out_specs=vmem,
        scratch=[
            pltpu.VMEM((2, 64, 64), f32),
            pltpu.VMEM((4, 128, 64), f32),
            pltpu.VMEM((8, 192, 64), f32),
            pltpu.VMEM((64, 192), f32),
            pltpu.VMEM((4, 64, 64), f32),
        ],
    )
    sent = call(outgoing, shape(16, ROWS), coefficients, factor3, own, got3, got)
    came = lax.ppermute(sent, PAIRS, RETURN)
    return call(staying, shape(16, ROWS), coefficients, factor3, own, got3, got, solves) + came


def solution(mesh):
    fine = Mesh(
        mesh.devices.reshape(4, 2, 2, 4, 2, 4), ("zl", "yh", "yl", "x", "core", "zh")
    )
    split_both = P("zh", BLOCKS)
    split_rows = P(None, BLOCKS)
    return jax.shard_map(
        on_device,
        mesh=fine,
        in_specs=(split_both,) * 4 + (split_rows,) * 3,
        out_specs=split_both,
        check_vma=False,
    )
```

```python
import functools

import jax
import jax.numpy as jnp
import numpy as np
from jax import lax
from jax.experimental import pallas as pl
from jax.experimental.pallas import tpu as pltpu
from jax.sharding import Mesh, PartitionSpec as P

RANK = 64
LOCAL = 16
ROWS = 4096
CHUNK = 2048
MESSAGE = 144
LIMIT = 48 * 1024 * 1024

LEAF = ("yl", "x", "core")
SLAB = ("yh", "zl", "zh")
BLOCKS = ("zl", "yh", "yl", "x", "core")
PAIRS = ("core", "zh")
SWAP = [(0, 1), (1, 0), (2, 3), (3, 2), (4, 7), (7, 4), (5, 6), (6, 5)]
RETURN = [(0, 3), (3, 0), (1, 2), (2, 1), (4, 5), (5, 4), (6, 7), (7, 6)]

bf16 = jnp.bfloat16
f32 = jnp.float32


def split(values):
    high = values.astype(bf16)
    return high, (values - high.astype(f32)).astype(bf16)


def dot(left, right):
    return jnp.dot(left, right, preferred_element_type=f32)


def exact(left, right):
    return full(left, right)


FREE = pl.CostEstimate(flops=0, bytes_accessed=0, transcendentals=0)


def full(left, right):
    count = left.shape[0]
    top, middle = split(left)
    low = (left - top.astype(f32) - middle.astype(f32)).astype(bf16)
    right_top, right_middle = split(right)
    right_low = (right - right_top.astype(f32) - right_middle.astype(f32)).astype(bf16)
    first = dot(jnp.concatenate([top, middle, low], 0), right_top)
    second = dot(jnp.concatenate([top, middle], 0), right_middle)
    third = dot(top, right_low)
    small = first[2 * count :] + second[count:] + third
    return first[:count] + (first[count : 2 * count] + second[:count] + small)


def products(
    solves, factor3, factor2, factor1, basis3, basis2, basis1, out, own, total3, total21
):
    step = pl.program_id(0)
    dims = (((1,), (1,)), ((), ()))
    factors = jnp.concatenate([factor2[...], factor1[...]], 0)
    own[...] = factors
    high, low = split(jnp.concatenate([solves[...], factor3[...], factors], 0))
    both = jnp.concatenate([high, low], 0)

    @pl.when(step == 0)
    def _():
        total3[...] = jnp.zeros_like(total3)
        total21[...] = jnp.zeros_like(total21)

    for total, basis in (
        (total3, basis3[...]),
        (total21, jnp.concatenate([basis2[...], basis1[...]], 0)),
    ):
        top, rest = split(basis)
        wide = lax.dot_general(both, top, dims, preferred_element_type=f32)
        thin = lax.dot_general(high, rest, dims, preferred_element_type=f32)
        total[...] += wide[:RANK] + (wide[RANK:] + thin)

    @pl.when(step == pl.num_programs(0) - 1)
    def _():
        deep = total3[...]
        pieces = [
            jnp.concatenate([deep[0:16], deep[32:48]], 1),
            jnp.concatenate([deep[16:32], deep[48:64]], 1),
            total21[16:32, :],
            total21[0:16, :],
            total21[32:48, :],
            total21[48:64, :],
            jnp.zeros((16, 128), f32),
            jnp.zeros((16, 128), f32),
        ]
        for index, piece in enumerate(pieces):
            out[:, 0, index, :] = piece[:8]
            out[:, 1, index, :] = piece[8:]


def local_products(*arrays):
    narrow = pl.BlockSpec((LOCAL, CHUNK), lambda i: (0, i))
    wide = pl.BlockSpec((RANK, CHUNK), lambda i: (0, i))
    return pl.pallas_call(
        products,
        grid=(ROWS // CHUNK,),
        in_specs=[narrow] * 4 + [wide] * 3,
        out_specs=(
            pl.BlockSpec((8, 2, 8, 128), lambda i: (0, 0, 0, 0)),
            pl.BlockSpec((2 * LOCAL, CHUNK), lambda i: (0, i)),
        ),
        out_shape=(shape(8, 2, 8, 128), shape(2 * LOCAL, ROWS)),
        scratch_shapes=[pltpu.VMEM((RANK, RANK), f32), pltpu.VMEM((RANK, 2 * RANK), f32)],
        cost_estimate=FREE,
    )(*arrays)


def leaf_sum(pieces, out):
    total = pieces[0]
    for index in range(1, 16):
        total = total + pieces[index]
    out[...] = jnp.broadcast_to(total[None], out.shape)


def pack(pieces, out):
    rows = [pieces[:, index, :] for index in range(6)]
    paired = [rows[index][:16] + rows[index][16:] for index in (3, 4, 5)]
    message = jnp.concatenate(rows[:3] + paired, 0)
    out[...] = jnp.broadcast_to(message[None], out.shape)


def identity():
    return (
        lax.broadcasted_iota(jnp.int32, (RANK, RANK), 0)
        == lax.broadcasted_iota(jnp.int32, (RANK, RANK), 1)
    ).astype(f32)


def squares(matrices):
    total = matrices[0] * matrices[0]
    for matrix in matrices[1:]:
        total = total + matrix * matrix
    return jnp.sum(total)


def inverses(crossed, scratch):
    eye = identity()
    seconds = [full(e, e) for e in crossed]
    close = squares(seconds) < 0.8

    @pl.when(close)
    def _():
        def improve(state):
            powers, guesses, _ = state
            both = [full(jnp.concatenate([p, g], 0), p) for g, p in zip(guesses, powers)]
            better = tuple(g + b[RANK:] for g, b in zip(guesses, both))
            higher = tuple(b[:RANK] for b in both)
            return higher, better, squares(powers)

        def unfinished(state):
            return state[2] > 1e-7

        state = lax.while_loop(
            unfinished,
            improve,
            (tuple(seconds), tuple(eye + e for e in crossed), jnp.float32(1.0)),
        )
        for index, guess in enumerate(state[1]):
            scratch[index] = guess

    @pl.when(jnp.logical_not(close))
    def _():
        matrices = [eye - e for e in crossed]
        starts = []
        for matrix in matrices:
            level = jnp.abs(matrix)
            by_row = jnp.max(jnp.sum(level, 1, keepdims=True), 0, keepdims=True)
            by_column = jnp.max(jnp.sum(level, 0, keepdims=True), 1, keepdims=True)
            starts.append(matrix.T / by_row / by_column)

        def improve(state):
            count, _, guesses = state
            gaps = [eye - exact(m, g) for m, g in zip(matrices, guesses)]
            better = tuple(g + exact(g, gap) for g, gap in zip(guesses, gaps))
            return count + 1, squares(gaps), better

        def unfinished(state):
            count, error, _ = state
            return (count < 64) & jnp.logical_not(error <= 1e-7)

        state = lax.while_loop(
            unfinished, improve, (jnp.int32(0), jnp.float32(1.0), tuple(starts))
        )
        for index, guess in enumerate(state[2]):
            scratch[index] = guess


def merge(nodes, scratch):
    crossed = [exact(kb, ka) for ka, kb, _, _ in nodes]
    sides = [ra - exact(rb, ka) for ka, _, ra, rb in nodes]
    inverses(crossed, scratch)
    bottoms = [exact(side, scratch[index]) for index, side in enumerate(sides)]
    tops = [rb - exact(low, kb) for (_, kb, _, rb), low in zip(nodes, bottoms)]
    return tops, bottoms


def tree(place, mine, other, out, first, second, third, whole, solved):
    first_core = place[5] == 0

    def rows(base, entry):
        parts = []
        for zh in range(4):
            here = pl.ds(base + entry * 4 + zh, 8, stride=MESSAGE)
            a, b = mine[here, :], other[here, :]
            parts += [jnp.where(first_core, a, b), jnp.where(first_core, b, a)]
        return jnp.concatenate(parts, 0)

    def left(values):
        return values[:, :RANK]

    def right(values):
        return values[:, RANK:]

    nodes = []
    couple = []
    carry = []
    for zl in range(4):
        xa, xb = rows(0, zl), rows(0, 4 + zl)
        fa, fb = rows(32, zl), rows(32, 4 + zl)
        nodes.append(
            (
                left(fa),
                left(fb),
                jnp.concatenate([left(xa), right(xa), right(fa)], 0),
                jnp.concatenate([left(xb), right(xb), right(fb)], 0),
            )
        )
        couple.append((rows(64, zl), rows(64, 4 + zl)))
        carry.append(jnp.concatenate([rows(96, zl), rows(112, zl), rows(128, zl)], 0))
    tops, bottoms = merge(nodes, solved)
    two = []
    one = []
    for zl in range(4):
        third[2 * zl] = tops[zl]
        third[2 * zl + 1] = bottoms[zl]
        update = exact(tops[zl], couple[zl][0]) + exact(bottoms[zl], couple[zl][1])
        carried = carry[zl] - update
        two.append(left(carried))
        one.append(right(carried))

    def keep(values):
        return jnp.concatenate([values[:RANK], values[2 * RANK :]], 0)

    nodes = [
        (
            two[2 * m][RANK : 2 * RANK],
            two[2 * m + 1][RANK : 2 * RANK],
            keep(two[2 * m]),
            keep(two[2 * m + 1]),
        )
        for m in range(2)
    ]
    tops, bottoms = merge(nodes, solved)
    last = []
    for m in range(2):
        second[2 * m] = tops[m]
        second[2 * m + 1] = bottoms[m]
        last.append(
            keep(one[2 * m])
            + keep(one[2 * m + 1])
            - exact(tops[m], one[2 * m][RANK : 2 * RANK])
            - exact(bottoms[m], one[2 * m + 1][RANK : 2 * RANK])
        )
    tops, bottoms = merge([(last[0][RANK:], last[1][RANK:], last[0][:RANK], last[1][:RANK])], solved)
    first[0] = tops[0]
    first[1] = bottoms[0]

    zl, yh, zh = place[0], place[1], place[2]
    partner = place[3]
    target = place[4]
    c3 = third[2 * zl + yh]
    c2 = second[zl]
    d1 = first[zl // 2]
    d2 = c2[:RANK] - exact(d1, c2[RANK:])
    d3 = c3[:RANK] - exact(d2, c3[RANK : 2 * RANK]) - exact(d1, c3[2 * RANK :])
    whole[...] = jnp.concatenate([d3, d2, d1], 1)

    picked = jnp.concatenate(
        [whole[pl.ds(zh * 16, 16), :], whole[pl.ds(target * 16, 16), :]], 0
    )
    source = lax.broadcasted_iota(jnp.int32, (192, 128), 0)
    column = lax.broadcasted_iota(jnp.int32, (192, 128), 1)
    owner = jnp.where(column < 48, zh, partner)
    inner = jnp.where(column < 48, column, column - 48)
    wanted = (inner // 16) * RANK + owner * 16 + inner % 16
    out[32:, :] = jnp.zeros((96, 128), f32)
    out[:32, :] = -exact(picked, ((source == wanted) & (column < 96)).astype(f32))


def apply_rows(coefficient, *factors):
    high, low = split(coefficient)
    both = jnp.concatenate([high, low], 0)
    top, rest = split(jnp.concatenate([factor[...] for factor in factors], 0))
    wide = dot(both, top)
    return wide[:16] + (wide[16:] + dot(high, rest))


def outgoing(weights, own3, own, got3, got, out):
    out[...] = apply_rows(weights[16:32, :96], own3, own, got3, got)


def staying(weights, own3, own, got3, got, solves, out):
    out[...] = solves[...] + apply_rows(weights[0:16, :96], own3, own, got3, got)


def call(kernel, shapes, *arrays, scratch=(), **kwargs):
    return pl.pallas_call(
        kernel,
        out_shape=shapes,
        scratch_shapes=list(scratch),
        compiler_params=pltpu.CompilerParams(vmem_limit_bytes=LIMIT),
        cost_estimate=FREE,
        **kwargs,
    )(*arrays)


def shape(*dims):
    return jax.ShapeDtypeStruct(dims, f32)


def on_device(solves, factor3, factor2, factor1, basis3, basis2, basis1):
    zh = lax.axis_index("zh")
    core = lax.axis_index("core")
    near, far = zh ^ 1, 3 - zh
    place = jnp.stack(
        [
            lax.axis_index("zl"),
            lax.axis_index("yh"),
            zh,
            jnp.where(core == 0, near, far),
            jnp.where(core == 0, far, near),
            core,
        ]
    ).astype(jnp.int32)
    got3 = lax.ppermute(factor3, PAIRS, SWAP)
    slots, own = local_products(solves, factor3, factor2, factor1, basis3, basis2, basis1)
    slots = slots.reshape(16, 8, 128)
    slots, place = lax.optimization_barrier((slots, place))
    pieces = lax.all_to_all(slots, LEAF, 0, 0, tiled=True)
    vmem = pl.BlockSpec(memory_space=pltpu.VMEM)

    copies = call(leaf_sum, shape(32, 8, 128), pieces)
    copies, got3 = lax.optimization_barrier((copies, got3))
    slabs = lax.all_to_all(copies, SLAB, 0, 0, tiled=True)
    slabs, own = lax.optimization_barrier((slabs, own))
    got = lax.ppermute(own, PAIRS, SWAP)

    def solve(_, state):
        message = call(pack, shape(8, MESSAGE, 128), slabs)
        mine = lax.all_to_all(message, ("yl", "x"), 0, 0, tiled=True).reshape(8 * MESSAGE, 128)
        other = lax.ppermute(mine, "core", [(0, 1), (1, 0)])
        return call(
            tree,
            shape(128, 128),
            place,
            mine,
            other,
            in_specs=[pl.BlockSpec(memory_space=pltpu.SMEM), vmem, vmem],
            out_specs=vmem,
            scratch=[
                pltpu.VMEM((2, 64, 64), f32),
                pltpu.VMEM((4, 128, 64), f32),
                pltpu.VMEM((8, 192, 64), f32),
                pltpu.VMEM((64, 192), f32),
                pltpu.VMEM((4, 64, 64), f32),
            ],
        )

    once = lax.optimization_barrier(jnp.int32(1))
    coefficients = lax.fori_loop(0, once, solve, pieces.reshape(128, 128))
    sent = call(outgoing, shape(16, ROWS), coefficients, factor3, own, got3, got)
    came = lax.ppermute(sent, PAIRS, RETURN)
    return call(staying, shape(16, ROWS), coefficients, factor3, own, got3, got, solves) + came


def solution(mesh):
    fine = Mesh(
        mesh.devices.reshape(4, 2, 2, 4, 2, 4), ("zl", "yh", "yl", "x", "core", "zh")
    )
    split_both = P("zh", BLOCKS)
    split_rows = P(None, BLOCKS)
    return jax.shard_map(
        on_device,
        mesh=fine,
        in_specs=(split_both,) * 4 + (split_rows,) * 3,
        out_specs=split_both,
        check_vma=False,
    )
```

```python
import functools

import jax
import jax.numpy as jnp
import numpy as np
from jax import lax
from jax.experimental import pallas as pl
from jax.experimental.pallas import tpu as pltpu
from jax.sharding import Mesh, PartitionSpec as P

RANK = 64
LOCAL = 16
ROWS = 4096
CHUNK = 2048
MESSAGE = 144
LIMIT = 48 * 1024 * 1024

LEAF = ("yl", "x", "core")
SLAB = ("yh", "zl", "zh")
BLOCKS = ("zl", "yh", "yl", "x", "core")
PAIRS = ("core", "zh")
SWAP = [(0, 1), (1, 0), (2, 3), (3, 2), (4, 7), (7, 4), (5, 6), (6, 5)]
RETURN = [(0, 3), (3, 0), (1, 2), (2, 1), (4, 5), (5, 4), (6, 7), (7, 6)]

bf16 = jnp.bfloat16
f32 = jnp.float32


def split(values):
    high = values.astype(bf16)
    return high, (values - high.astype(f32)).astype(bf16)


def dot(left, right):
    return jnp.dot(left, right, preferred_element_type=f32)


def exact(left, right):
    count = left.shape[0]
    top, middle = split(left)
    right_top, right_middle = split(right)
    first = dot(jnp.concatenate([top, middle], 0), right_top)
    return first[:count] + (first[count:] + dot(top, right_middle))


FREE = pl.CostEstimate(flops=0, bytes_accessed=0, transcendentals=0)


def full(left, right):
    count = left.shape[0]
    top, middle = split(left)
    low = (left - top.astype(f32) - middle.astype(f32)).astype(bf16)
    right_top, right_middle = split(right)
    right_low = (right - right_top.astype(f32) - right_middle.astype(f32)).astype(bf16)
    first = dot(jnp.concatenate([top, middle, low], 0), right_top)
    second = dot(jnp.concatenate([top, middle], 0), right_middle)
    third = dot(top, right_low)
    small = first[2 * count :] + second[count:] + third
    return first[:count] + (first[count : 2 * count] + second[:count] + small)


def products(
    solves, factor3, factor2, factor1, basis3, basis2, basis1, out, own, total3, total21
):
    step = pl.program_id(0)
    dims = (((1,), (1,)), ((), ()))
    factors = jnp.concatenate([factor2[...], factor1[...]], 0)
    own[...] = factors
    high, low = split(jnp.concatenate([solves[...], factor3[...], factors], 0))
    both = jnp.concatenate([high, low], 0)

    @pl.when(step == 0)
    def _():
        total3[...] = jnp.zeros_like(total3)
        total21[...] = jnp.zeros_like(total21)

    for total, basis in (
        (total3, basis3[...]),
        (total21, jnp.concatenate([basis2[...], basis1[...]], 0)),
    ):
        top, rest = split(basis)
        wide = lax.dot_general(both, top, dims, preferred_element_type=f32)
        thin = lax.dot_general(high, rest, dims, preferred_element_type=f32)
        total[...] += wide[:RANK] + (wide[RANK:] + thin)

    @pl.when(step == pl.num_programs(0) - 1)
    def _():
        deep = total3[...]
        pieces = [
            jnp.concatenate([deep[0:16], deep[32:48]], 1),
            jnp.concatenate([deep[16:32], deep[48:64]], 1),
            total21[16:32, :],
            total21[0:16, :],
            total21[32:48, :],
            total21[48:64, :],
            jnp.zeros((16, 128), f32),
            jnp.zeros((16, 128), f32),
        ]
        for index, piece in enumerate(pieces):
            out[:, 0, index, :] = piece[:8]
            out[:, 1, index, :] = piece[8:]


def local_products(*arrays):
    narrow = pl.BlockSpec((LOCAL, CHUNK), lambda i: (0, i))
    wide = pl.BlockSpec((RANK, CHUNK), lambda i: (0, i))
    return pl.pallas_call(
        products,
        grid=(ROWS // CHUNK,),
        in_specs=[narrow] * 4 + [wide] * 3,
        out_specs=(
            pl.BlockSpec((8, 2, 8, 128), lambda i: (0, 0, 0, 0)),
            pl.BlockSpec((2 * LOCAL, CHUNK), lambda i: (0, i)),
        ),
        out_shape=(shape(8, 2, 8, 128), shape(2 * LOCAL, ROWS)),
        scratch_shapes=[pltpu.VMEM((RANK, RANK), f32), pltpu.VMEM((RANK, 2 * RANK), f32)],
        cost_estimate=FREE,
    )(*arrays)


def leaf_sum(pieces, out):
    total = pieces[0]
    for index in range(1, 16):
        total = total + pieces[index]
    out[...] = jnp.broadcast_to(total[None], out.shape)


def pack(pieces, out):
    rows = [pieces[:, index, :] for index in range(6)]
    paired = [rows[index][:16] + rows[index][16:] for index in (3, 4, 5)]
    message = jnp.concatenate(rows[:3] + paired, 0)
    out[...] = jnp.broadcast_to(message[None], out.shape)


def identity():
    return (
        lax.broadcasted_iota(jnp.int32, (RANK, RANK), 0)
        == lax.broadcasted_iota(jnp.int32, (RANK, RANK), 1)
    ).astype(f32)


def squares(matrices):
    total = matrices[0] * matrices[0]
    for matrix in matrices[1:]:
        total = total + matrix * matrix
    return jnp.sum(total)


def inverses(crossed, scratch):
    eye = identity()
    seconds = [full(e, e) for e in crossed]
    close = squares(seconds) < 0.8

    @pl.when(close)
    def _():
        def improve(state):
            powers, guesses, _ = state
            both = [full(jnp.concatenate([p, g], 0), p) for g, p in zip(guesses, powers)]
            better = tuple(g + b[RANK:] for g, b in zip(guesses, both))
            higher = tuple(b[:RANK] for b in both)
            return higher, better, squares(powers)

        def unfinished(state):
            return state[2] > 2e-6

        state = lax.while_loop(
            unfinished,
            improve,
            (tuple(seconds), tuple(eye + e for e in crossed), jnp.float32(1.0)),
        )
        for index, guess in enumerate(state[1]):
            scratch[index] = guess

    @pl.when(jnp.logical_not(close))
    def _():
        matrices = [eye - e for e in crossed]
        starts = []
        for matrix in matrices:
            level = jnp.abs(matrix)
            by_row = jnp.max(jnp.sum(level, 1, keepdims=True), 0, keepdims=True)
            by_column = jnp.max(jnp.sum(level, 0, keepdims=True), 1, keepdims=True)
            starts.append(matrix.T / by_row / by_column)

        def improve(state):
            count, _, guesses = state
            gaps = [eye - exact(m, g) for m, g in zip(matrices, guesses)]
            better = tuple(g + exact(g, gap) for g, gap in zip(guesses, gaps))
            return count + 1, squares(gaps), better

        def unfinished(state):
            count, error, _ = state
            return (count < 64) & jnp.logical_not(error <= 1e-7)

        state = lax.while_loop(
            unfinished, improve, (jnp.int32(0), jnp.float32(1.0), tuple(starts))
        )
        for index, guess in enumerate(state[2]):
            scratch[index] = guess


def merge(nodes, scratch, couples=()):
    crossed = [full(kb, ka) for ka, kb, _, _ in nodes]
    sides = [ra - exact(rb, ka) for ka, _, ra, rb in nodes]
    known = [exact(node[3], ca) for node, (ca, _) in zip(nodes, couples)]
    gains = [cb - exact(node[1], ca) for node, (ca, cb) in zip(nodes, couples)]
    inverses(crossed, scratch)
    bottoms = [exact(side, scratch[index]) for index, side in enumerate(sides)]
    tops = [rb - exact(low, kb) for (_, kb, _, rb), low in zip(nodes, bottoms)]
    updates = [first + exact(low, gain) for first, low, gain in zip(known, bottoms, gains)]
    return tops, bottoms, updates


def tree(place, mine, other, out, first, second, third, whole, solved):
    first_core = place[5] == 0

    def rows(base, entry):
        parts = []
        for zh in range(4):
            here = pl.ds(base + entry * 4 + zh, 8, stride=MESSAGE)
            a, b = mine[here, :], other[here, :]
            parts += [jnp.where(first_core, a, b), jnp.where(first_core, b, a)]
        return jnp.concatenate(parts, 0)

    def left(values):
        return values[:, :RANK]

    def right(values):
        return values[:, RANK:]

    nodes = []
    couple = []
    carry = []
    for zl in range(4):
        xa, xb = rows(0, zl), rows(0, 4 + zl)
        fa, fb = rows(32, zl), rows(32, 4 + zl)
        nodes.append(
            (
                left(fa),
                left(fb),
                jnp.concatenate([left(xa), right(xa), right(fa)], 0),
                jnp.concatenate([left(xb), right(xb), right(fb)], 0),
            )
        )
        couple.append((rows(64, zl), rows(64, 4 + zl)))
        carry.append(jnp.concatenate([rows(96, zl), rows(112, zl), rows(128, zl)], 0))
    tops, bottoms, updates = merge(nodes, solved, couple)
    two = []
    one = []
    for zl in range(4):
        third[2 * zl] = tops[zl]
        third[2 * zl + 1] = bottoms[zl]
        carried = carry[zl] - updates[zl]
        two.append(left(carried))
        one.append(right(carried))

    def keep(values):
        return jnp.concatenate([values[:RANK], values[2 * RANK :]], 0)

    nodes = [
        (
            two[2 * m][RANK : 2 * RANK],
            two[2 * m + 1][RANK : 2 * RANK],
            keep(two[2 * m]),
            keep(two[2 * m + 1]),
        )
        for m in range(2)
    ]
    middle = [values[RANK : 2 * RANK] for values in one]
    tops, bottoms, updates = merge(nodes, solved, [middle[:2], middle[2:]])
    last = []
    for m in range(2):
        second[2 * m] = tops[m]
        second[2 * m + 1] = bottoms[m]
        last.append(keep(one[2 * m]) + keep(one[2 * m + 1]) - updates[m])
    node = (last[0][RANK:], last[1][RANK:], last[0][:RANK], last[1][:RANK])
    tops, bottoms, _ = merge([node], solved)
    first[0] = tops[0]
    first[1] = bottoms[0]

    zl, yh, zh = place[0], place[1], place[2]
    partner = place[3]
    target = place[4]
    c3 = third[2 * zl + yh]
    c2 = second[zl]
    d1 = first[zl // 2]
    d2 = c2[:RANK] - exact(d1, c2[RANK:])
    d3 = c3[:RANK] - exact(d2, c3[RANK : 2 * RANK]) - exact(d1, c3[2 * RANK :])
    whole[...] = jnp.concatenate([d3, d2, d1], 1)

    picked = jnp.concatenate(
        [whole[pl.ds(zh * 16, 16), :], whole[pl.ds(target * 16, 16), :]], 0
    )
    source = lax.broadcasted_iota(jnp.int32, (192, 128), 0)
    column = lax.broadcasted_iota(jnp.int32, (192, 128), 1)
    owner = jnp.where(column < 48, zh, partner)
    inner = jnp.where(column < 48, column, column - 48)
    wanted = (inner // 16) * RANK + owner * 16 + inner % 16
    out[32:, :] = jnp.zeros((96, 128), f32)
    out[:32, :] = -exact(picked, ((source == wanted) & (column < 96)).astype(f32))


def apply_rows(coefficient, *factors):
    high, low = split(coefficient)
    both = jnp.concatenate([high, low], 0)
    top, rest = split(jnp.concatenate([factor[...] for factor in factors], 0))
    wide = dot(both, top)
    return wide[:16] + (wide[16:] + dot(high, rest))


def outgoing(weights, own3, own, got3, got, out):
    out[...] = apply_rows(weights[16:32, :96], own3, own, got3, got)


def staying(weights, own3, own, got3, got, solves, out):
    out[...] = solves[...] + apply_rows(weights[0:16, :96], own3, own, got3, got)


def call(kernel, shapes, *arrays, scratch=(), **kwargs):
    return pl.pallas_call(
        kernel,
        out_shape=shapes,
        scratch_shapes=list(scratch),
        compiler_params=pltpu.CompilerParams(vmem_limit_bytes=LIMIT),
        cost_estimate=FREE,
        **kwargs,
    )(*arrays)


def shape(*dims):
    return jax.ShapeDtypeStruct(dims, f32)


def on_device(solves, factor3, factor2, factor1, basis3, basis2, basis1):
    zh = lax.axis_index("zh")
    core = lax.axis_index("core")
    near, far = zh ^ 1, 3 - zh
    place = jnp.stack(
        [
            lax.axis_index("zl"),
            lax.axis_index("yh"),
            zh,
            jnp.where(core == 0, near, far),
            jnp.where(core == 0, far, near),
            core,
        ]
    ).astype(jnp.int32)
    got3 = lax.ppermute(factor3, PAIRS, SWAP)
    slots, own = local_products(solves, factor3, factor2, factor1, basis3, basis2, basis1)
    slots = slots.reshape(16, 8, 128)
    slots, place = lax.optimization_barrier((slots, place))
    pieces = lax.all_to_all(slots, LEAF, 0, 0, tiled=True)
    vmem = pl.BlockSpec(memory_space=pltpu.VMEM)

    copies = call(leaf_sum, shape(32, 8, 128), pieces)
    copies, got3 = lax.optimization_barrier((copies, got3))
    slabs = lax.all_to_all(copies, SLAB, 0, 0, tiled=True)
    slabs, own = lax.optimization_barrier((slabs, own))
    got = lax.ppermute(own, PAIRS, SWAP)

    def solve():
        message = call(pack, shape(8, MESSAGE, 128), slabs)
        mine = lax.all_to_all(message, ("yl", "x"), 0, 0, tiled=True).reshape(8 * MESSAGE, 128)
        other = lax.ppermute(mine, "core", [(0, 1), (1, 0)])
        return call(
            tree,
            shape(128, 128),
            place,
            mine,
            other,
            in_specs=[pl.BlockSpec(memory_space=pltpu.SMEM), vmem, vmem],
            out_specs=vmem,
            scratch=[
                pltpu.VMEM((2, 64, 64), f32),
                pltpu.VMEM((4, 128, 64), f32),
                pltpu.VMEM((8, 192, 64), f32),
                pltpu.VMEM((64, 192), f32),
                pltpu.VMEM((4, 64, 64), f32),
            ],
        )

    once = lax.optimization_barrier(jnp.int32(1))
    coefficients = lax.cond(once > 0, solve, lambda: jnp.zeros((128, 128), f32))
    sent = call(outgoing, shape(16, ROWS), coefficients, factor3, own, got3, got)
    came = lax.ppermute(sent, PAIRS, RETURN)
    return call(staying, shape(16, ROWS), coefficients, factor3, own, got3, got, solves) + came


def solution(mesh):
    fine = Mesh(
        mesh.devices.reshape(4, 2, 2, 4, 2, 4), ("zl", "yh", "yl", "x", "core", "zh")
    )
    split_both = P("zh", BLOCKS)
    split_rows = P(None, BLOCKS)
    return jax.shard_map(
        on_device,
        mesh=fine,
        in_specs=(split_both,) * 4 + (split_rows,) * 3,
        out_specs=split_both,
        check_vma=False,
    )
```

```python
import functools

import jax
import jax.numpy as jnp
import numpy as np
from jax import lax
from jax.experimental import pallas as pl
from jax.experimental.pallas import tpu as pltpu
from jax.sharding import Mesh, PartitionSpec as P

RANK = 64
LOCAL = 16
ROWS = 4096
CHUNK = 2048
MESSAGE = 144
LIMIT = 48 * 1024 * 1024

LEAF = ("yl", "x", "core")
SLAB = ("yh", "zl", "zh")
BLOCKS = ("zl", "yh", "yl", "x", "core")
PAIRS = ("core", "zh")
SWAP = [(0, 1), (1, 0), (2, 3), (3, 2), (4, 7), (7, 4), (5, 6), (6, 5)]
RETURN = [(0, 3), (3, 0), (1, 2), (2, 1), (4, 5), (5, 4), (6, 7), (7, 6)]

bf16 = jnp.bfloat16
f32 = jnp.float32


def split(values):
    high = values.astype(bf16)
    return high, (values - high.astype(f32)).astype(bf16)


def dot(left, right):
    return jnp.dot(left, right, preferred_element_type=f32)


def exact(left, right):
    count = left.shape[0]
    top, middle = split(left)
    right_top, right_middle = split(right)
    first = dot(jnp.concatenate([top, middle], 0), right_top)
    return first[:count] + (first[count:] + dot(top, right_middle))


FREE = pl.CostEstimate(flops=0, bytes_accessed=0, transcendentals=0)


def full(left, right):
    count = left.shape[0]
    top, middle = split(left)
    low = (left - top.astype(f32) - middle.astype(f32)).astype(bf16)
    right_top, right_middle = split(right)
    right_low = (right - right_top.astype(f32) - right_middle.astype(f32)).astype(bf16)
    first = dot(jnp.concatenate([top, middle, low], 0), right_top)
    second = dot(jnp.concatenate([top, middle], 0), right_middle)
    third = dot(top, right_low)
    small = first[2 * count :] + second[count:] + third
    return first[:count] + (first[count : 2 * count] + second[:count] + small)


def products(
    solves, factor3, factor2, factor1, basis3, basis2, basis1, out, own, stacked, bases, sems, done
):
    dims = (((1,), (1,)), ((), ()))
    sources = (solves, factor3, factor2, factor1, basis3, basis2, basis1)
    starts = (0, 16, 32, 48, 0, 64, 128)
    copies = []
    for chunk in range(ROWS // CHUNK):
        columns = pl.ds(chunk * CHUNK, CHUNK)
        row = []
        for index, (source, start) in enumerate(zip(sources, starts)):
            target = stacked if index < 4 else bases
            rows = pl.ds(start, source.shape[0])
            row.append(
                pltpu.make_async_copy(
                    source.at[:, columns], target.at[rows, columns], sems.at[chunk, index]
                )
            )
        copies.append(row)
    for row in copies:
        for copy in row:
            copy.start()
    leaving = pltpu.make_async_copy(stacked.at[pl.ds(2 * LOCAL, 2 * LOCAL), :], own, done)
    deep = jnp.zeros((RANK, RANK), f32)
    wide = jnp.zeros((RANK, 2 * RANK), f32)
    for chunk, row in enumerate(copies):
        for copy in row:
            copy.wait()
        if chunk == ROWS // CHUNK - 1:
            leaving.start()
        columns = slice(chunk * CHUNK, (chunk + 1) * CHUNK)
        high, low = split(stacked[:, columns])
        both = jnp.concatenate([high, low], 0)
        sums = []
        for basis in (bases[:RANK, columns], bases[RANK:, columns]):
            top, rest = split(basis)
            main = lax.dot_general(both, top, dims, preferred_element_type=f32)
            thin = lax.dot_general(high, rest, dims, preferred_element_type=f32)
            sums.append(main[:RANK] + (main[RANK:] + thin))
        deep = deep + sums[0]
        wide = wide + sums[1]
    pieces = [
        jnp.concatenate([deep[0:16], deep[32:48]], 1),
        jnp.concatenate([deep[16:32], deep[48:64]], 1),
        wide[16:32, :],
        wide[0:16, :],
        wide[32:48, :],
        wide[48:64, :],
        jnp.zeros((16, 128), f32),
        jnp.zeros((16, 128), f32),
    ]
    for index, piece in enumerate(pieces):
        out[:, 0, index, :] = piece[:8]
        out[:, 1, index, :] = piece[8:]
    leaving.wait()


def local_products(*arrays):
    anywhere = pl.BlockSpec(memory_space=pl.ANY)
    return pl.pallas_call(
        products,
        in_specs=[anywhere] * 7,
        out_specs=(pl.BlockSpec(memory_space=pltpu.VMEM), anywhere),
        out_shape=(shape(8, 2, 8, 128), shape(2 * LOCAL, ROWS)),
        scratch_shapes=[
            pltpu.VMEM((RANK, ROWS), f32),
            pltpu.VMEM((3 * RANK, ROWS), f32),
            pltpu.SemaphoreType.DMA((ROWS // CHUNK, 7)),
            pltpu.SemaphoreType.DMA,
        ],
        cost_estimate=FREE,
    )(*arrays)


def leaf_sum(pieces, out):
    total = pieces[0]
    for index in range(1, 16):
        total = total + pieces[index]
    out[...] = jnp.broadcast_to(total[None], out.shape)


def pack(pieces, out):
    rows = [pieces[:, index, :] for index in range(6)]
    paired = [rows[index][:16] + rows[index][16:] for index in (3, 4, 5)]
    message = jnp.concatenate(rows[:3] + paired, 0)
    out[...] = jnp.broadcast_to(message[None], out.shape)


def identity():
    return (
        lax.broadcasted_iota(jnp.int32, (RANK, RANK), 0)
        == lax.broadcasted_iota(jnp.int32, (RANK, RANK), 1)
    ).astype(f32)


def squares(matrices):
    total = matrices[0] * matrices[0]
    for matrix in matrices[1:]:
        total = total + matrix * matrix
    return jnp.sum(total)


def inverses(crossed, scratch):
    eye = identity()
    seconds = [full(e, e) for e in crossed]
    close = squares(seconds) < 0.8

    @pl.when(close)
    def _():
        def improve(state):
            powers, guesses, _ = state
            both = [full(jnp.concatenate([p, g], 0), p) for g, p in zip(guesses, powers)]
            better = tuple(g + b[RANK:] for g, b in zip(guesses, both))
            higher = tuple(b[:RANK] for b in both)
            return higher, better, squares(powers)

        def unfinished(state):
            return state[2] > 2e-6

        state = lax.while_loop(
            unfinished,
            improve,
            (tuple(seconds), tuple(eye + e for e in crossed), jnp.float32(1.0)),
        )
        for index, guess in enumerate(state[1]):
            scratch[index] = guess

    @pl.when(jnp.logical_not(close))
    def _():
        matrices = [eye - e for e in crossed]
        starts = []
        for matrix in matrices:
            level = jnp.abs(matrix)
            by_row = jnp.max(jnp.sum(level, 1, keepdims=True), 0, keepdims=True)
            by_column = jnp.max(jnp.sum(level, 0, keepdims=True), 1, keepdims=True)
            starts.append(matrix.T / by_row / by_column)

        def improve(state):
            count, _, guesses = state
            gaps = [eye - exact(m, g) for m, g in zip(matrices, guesses)]
            better = tuple(g + exact(g, gap) for g, gap in zip(guesses, gaps))
            return count + 1, squares(gaps), better

        def unfinished(state):
            count, error, _ = state
            return (count < 64) & jnp.logical_not(error <= 1e-7)

        state = lax.while_loop(
            unfinished, improve, (jnp.int32(0), jnp.float32(1.0), tuple(starts))
        )
        for index, guess in enumerate(state[2]):
            scratch[index] = guess


def merge(nodes, scratch, couples=()):
    crossed = [full(kb, ka) for ka, kb, _, _ in nodes]
    sides = [ra - exact(rb, ka) for ka, _, ra, rb in nodes]
    known = [exact(node[3], ca) for node, (ca, _) in zip(nodes, couples)]
    gains = [cb - exact(node[1], ca) for node, (ca, cb) in zip(nodes, couples)]
    inverses(crossed, scratch)
    bottoms = [exact(side, scratch[index]) for index, side in enumerate(sides)]
    tops = [rb - exact(low, kb) for (_, kb, _, rb), low in zip(nodes, bottoms)]
    updates = [first + exact(low, gain) for first, low, gain in zip(known, bottoms, gains)]
    return tops, bottoms, updates


def tree(place, mine, other, out, first, second, third, whole, solved):
    first_core = place[5] == 0

    def rows(base, entry):
        parts = []
        for zh in range(4):
            here = pl.ds(base + entry * 4 + zh, 8, stride=MESSAGE)
            a, b = mine[here, :], other[here, :]
            parts += [jnp.where(first_core, a, b), jnp.where(first_core, b, a)]
        return jnp.concatenate(parts, 0)

    def left(values):
        return values[:, :RANK]

    def right(values):
        return values[:, RANK:]

    nodes = []
    couple = []
    carry = []
    for zl in range(4):
        xa, xb = rows(0, zl), rows(0, 4 + zl)
        fa, fb = rows(32, zl), rows(32, 4 + zl)
        nodes.append(
            (
                left(fa),
                left(fb),
                jnp.concatenate([left(xa), right(xa), right(fa)], 0),
                jnp.concatenate([left(xb), right(xb), right(fb)], 0),
            )
        )
        couple.append((rows(64, zl), rows(64, 4 + zl)))
        carry.append(jnp.concatenate([rows(96, zl), rows(112, zl), rows(128, zl)], 0))
    tops, bottoms, updates = merge(nodes, solved, couple)
    two = []
    one = []
    for zl in range(4):
        third[2 * zl] = tops[zl]
        third[2 * zl + 1] = bottoms[zl]
        carried = carry[zl] - updates[zl]
        two.append(left(carried))
        one.append(right(carried))

    def keep(values):
        return jnp.concatenate([values[:RANK], values[2 * RANK :]], 0)

    nodes = [
        (
            two[2 * m][RANK : 2 * RANK],
            two[2 * m + 1][RANK : 2 * RANK],
            keep(two[2 * m]),
            keep(two[2 * m + 1]),
        )
        for m in range(2)
    ]
    middle = [values[RANK : 2 * RANK] for values in one]
    tops, bottoms, updates = merge(nodes, solved, [middle[:2], middle[2:]])
    last = []
    for m in range(2):
        second[2 * m] = tops[m]
        second[2 * m + 1] = bottoms[m]
        last.append(keep(one[2 * m]) + keep(one[2 * m + 1]) - updates[m])
    node = (last[0][RANK:], last[1][RANK:], last[0][:RANK], last[1][:RANK])
    tops, bottoms, _ = merge([node], solved)
    first[0] = tops[0]
    first[1] = bottoms[0]

    zl, yh, zh = place[0], place[1], place[2]
    partner = place[3]
    target = place[4]
    c3 = third[2 * zl + yh]
    c2 = second[zl]
    d1 = first[zl // 2]
    d2 = c2[:RANK] - exact(d1, c2[RANK:])
    d3 = c3[:RANK] - exact(d2, c3[RANK : 2 * RANK]) - exact(d1, c3[2 * RANK :])
    whole[...] = jnp.concatenate([d3, d2, d1], 1)

    picked = jnp.concatenate(
        [whole[pl.ds(zh * 16, 16), :], whole[pl.ds(target * 16, 16), :]], 0
    )
    source = lax.broadcasted_iota(jnp.int32, (192, 128), 0)
    column = lax.broadcasted_iota(jnp.int32, (192, 128), 1)
    owner = jnp.where(column < 48, zh, partner)
    inner = jnp.where(column < 48, column, column - 48)
    wanted = (inner // 16) * RANK + owner * 16 + inner % 16
    out[32:, :] = jnp.zeros((96, 128), f32)
    out[:32, :] = -exact(picked, ((source == wanted) & (column < 96)).astype(f32))


def apply_rows(coefficient, *factors):
    high, low = split(coefficient)
    both = jnp.concatenate([high, low], 0)
    top, rest = split(jnp.concatenate([factor[...] for factor in factors], 0))
    wide = dot(both, top)
    return wide[:16] + (wide[16:] + dot(high, rest))


def outgoing(weights, own3, own, got3, got, out):
    out[...] = apply_rows(weights[16:32, :96], own3, own, got3, got)


def staying(weights, own3, own, got3, got, solves, out):
    out[...] = solves[...] + apply_rows(weights[0:16, :96], own3, own, got3, got)


def call(kernel, shapes, *arrays, scratch=(), **kwargs):
    return pl.pallas_call(
        kernel,
        out_shape=shapes,
        scratch_shapes=list(scratch),
        compiler_params=pltpu.CompilerParams(vmem_limit_bytes=LIMIT),
        cost_estimate=FREE,
        **kwargs,
    )(*arrays)


def shape(*dims):
    return jax.ShapeDtypeStruct(dims, f32)


def on_device(solves, factor3, factor2, factor1, basis3, basis2, basis1):
    zh = lax.axis_index("zh")
    core = lax.axis_index("core")
    near, far = zh ^ 1, 3 - zh
    place = jnp.stack(
        [
            lax.axis_index("zl"),
            lax.axis_index("yh"),
            zh,
            jnp.where(core == 0, near, far),
            jnp.where(core == 0, far, near),
            core,
        ]
    ).astype(jnp.int32)
    got3 = lax.ppermute(factor3, PAIRS, SWAP)
    slots, own = local_products(solves, factor3, factor2, factor1, basis3, basis2, basis1)
    slots = slots.reshape(16, 8, 128)
    slots, place = lax.optimization_barrier((slots, place))
    pieces = lax.all_to_all(slots, LEAF, 0, 0, tiled=True)
    vmem = pl.BlockSpec(memory_space=pltpu.VMEM)

    copies = call(leaf_sum, shape(32, 8, 128), pieces)
    copies, got3 = lax.optimization_barrier((copies, got3))
    slabs = lax.all_to_all(copies, SLAB, 0, 0, tiled=True)
    slabs, own = lax.optimization_barrier((slabs, own))
    got = lax.ppermute(own, PAIRS, SWAP)

    def solve():
        message = call(pack, shape(8, MESSAGE, 128), slabs)
        mine = lax.all_to_all(message, ("yl", "x"), 0, 0, tiled=True).reshape(8 * MESSAGE, 128)
        other = lax.ppermute(mine, "core", [(0, 1), (1, 0)])
        return call(
            tree,
            shape(128, 128),
            place,
            mine,
            other,
            in_specs=[pl.BlockSpec(memory_space=pltpu.SMEM), vmem, vmem],
            out_specs=vmem,
            scratch=[
                pltpu.VMEM((2, 64, 64), f32),
                pltpu.VMEM((4, 128, 64), f32),
                pltpu.VMEM((8, 192, 64), f32),
                pltpu.VMEM((64, 192), f32),
                pltpu.VMEM((4, 64, 64), f32),
            ],
        )

    once = lax.optimization_barrier(jnp.int32(1))
    coefficients = lax.cond(once > 0, solve, lambda: jnp.zeros((128, 128), f32))
    sent = call(outgoing, shape(16, ROWS), coefficients, factor3, own, got3, got)
    came = lax.ppermute(sent, PAIRS, RETURN)
    return call(staying, shape(16, ROWS), coefficients, factor3, own, got3, got, solves) + came


def solution(mesh):
    fine = Mesh(
        mesh.devices.reshape(4, 2, 2, 4, 2, 4), ("zl", "yh", "yl", "x", "core", "zh")
    )
    split_both = P("zh", BLOCKS)
    split_rows = P(None, BLOCKS)
    return jax.shard_map(
        on_device,
        mesh=fine,
        in_specs=(split_both,) * 4 + (split_rows,) * 3,
        out_specs=split_both,
        check_vma=False,
    )
```

```python
import functools

import jax
import jax.numpy as jnp
import numpy as np
from jax import lax
from jax.experimental import pallas as pl
from jax.experimental.pallas import tpu as pltpu
from jax.sharding import Mesh, PartitionSpec as P

RANK = 64
LOCAL = 16
ROWS = 4096
CHUNK = 2048
MESSAGE = 144
LIMIT = 48 * 1024 * 1024

LEAF = ("yl", "x", "core")
SLAB = ("yh", "zl", "zh")
BLOCKS = ("zl", "yh", "yl", "x", "core")
PAIRS = ("core", "zh")
SWAP = [(0, 1), (1, 0), (2, 3), (3, 2), (4, 7), (7, 4), (5, 6), (6, 5)]
RETURN = [(0, 3), (3, 0), (1, 2), (2, 1), (4, 5), (5, 4), (6, 7), (7, 6)]

bf16 = jnp.bfloat16
f32 = jnp.float32


def split(values):
    high = values.astype(bf16)
    return high, (values - high.astype(f32)).astype(bf16)


def dot(left, right):
    return jnp.dot(left, right, preferred_element_type=f32)


def exact(left, right):
    count = left.shape[0]
    top, middle = split(left)
    right_top, right_middle = split(right)
    first = dot(jnp.concatenate([top, middle], 0), right_top)
    return first[:count] + (first[count:] + dot(top, right_middle))


FREE = pl.CostEstimate(flops=0, bytes_accessed=0, transcendentals=0)


def full(left, right):
    count = left.shape[0]
    top, middle = split(left)
    low = (left - top.astype(f32) - middle.astype(f32)).astype(bf16)
    right_top, right_middle = split(right)
    right_low = (right - right_top.astype(f32) - right_middle.astype(f32)).astype(bf16)
    first = dot(jnp.concatenate([top, middle, low], 0), right_top)
    second = dot(jnp.concatenate([top, middle], 0), right_middle)
    third = dot(top, right_low)
    small = first[2 * count :] + second[count:] + third
    return first[:count] + (first[count : 2 * count] + second[:count] + small)


def products(
    solves, factor3, factor2, factor1, basis3, basis2, basis1, out, own, total3, total21
):
    step = pl.program_id(0)
    dims = (((1,), (1,)), ((), ()))
    factors = jnp.concatenate([factor2[...], factor1[...]], 0)
    own[...] = factors
    high, low = split(jnp.concatenate([solves[...], factor3[...], factors], 0))
    both = jnp.concatenate([high, low], 0)

    @pl.when(step == 0)
    def _():
        total3[...] = jnp.zeros_like(total3)
        total21[...] = jnp.zeros_like(total21)

    for total, basis in (
        (total3, basis3[...]),
        (total21, jnp.concatenate([basis2[...], basis1[...]], 0)),
    ):
        top, rest = split(basis)
        wide = lax.dot_general(both, top, dims, preferred_element_type=f32)
        thin = lax.dot_general(high, rest, dims, preferred_element_type=f32)
        total[...] += wide[:RANK] + (wide[RANK:] + thin)

    @pl.when(step == pl.num_programs(0) - 1)
    def _():
        deep = total3[...]
        pieces = [
            jnp.concatenate([deep[0:16], deep[32:48]], 1),
            jnp.concatenate([deep[16:32], deep[48:64]], 1),
            total21[16:32, :],
            total21[0:16, :],
            total21[32:48, :],
            total21[48:64, :],
            jnp.zeros((16, 128), f32),
            jnp.zeros((16, 128), f32),
        ]
        for index, piece in enumerate(pieces):
            out[:, 0, index, :] = piece[:8]
            out[:, 1, index, :] = piece[8:]


def local_products(*arrays):
    narrow = pl.BlockSpec((LOCAL, CHUNK), lambda i: (0, i))
    wide = pl.BlockSpec((RANK, CHUNK), lambda i: (0, i))
    return pl.pallas_call(
        products,
        grid=(ROWS // CHUNK,),
        in_specs=[narrow] * 4 + [wide] * 3,
        out_specs=(
            pl.BlockSpec((8, 2, 8, 128), lambda i: (0, 0, 0, 0)),
            pl.BlockSpec((2 * LOCAL, CHUNK), lambda i: (0, i)),
        ),
        out_shape=(shape(8, 2, 8, 128), shape(2 * LOCAL, ROWS)),
        scratch_shapes=[pltpu.VMEM((RANK, RANK), f32), pltpu.VMEM((RANK, 2 * RANK), f32)],
        cost_estimate=FREE,
    )(*arrays)


def leaf_sum(pieces, out):
    total = pieces[0]
    for index in range(1, 16):
        total = total + pieces[index]
    out[...] = jnp.broadcast_to(total[None], out.shape)


def pack(pieces, out):
    rows = [pieces[:, index, :] for index in range(6)]
    paired = [rows[index][:16] + rows[index][16:] for index in (3, 4, 5)]
    message = jnp.concatenate(rows[:3] + paired, 0)
    out[...] = jnp.broadcast_to(message[None], out.shape)


def identity():
    return (
        lax.broadcasted_iota(jnp.int32, (RANK, RANK), 0)
        == lax.broadcasted_iota(jnp.int32, (RANK, RANK), 1)
    ).astype(f32)


def squares(matrices):
    total = matrices[0] * matrices[0]
    for matrix in matrices[1:]:
        total = total + matrix * matrix
    return jnp.sum(total)


def inverses(crossed, scratch):
    eye = identity()
    seconds = [full(e, e) for e in crossed]
    close = squares(seconds) < 0.8

    @pl.when(close)
    def _():
        def improve(state):
            powers, guesses, _ = state
            both = [full(jnp.concatenate([p, g], 0), p) for g, p in zip(guesses, powers)]
            better = tuple(g + b[RANK:] for g, b in zip(guesses, both))
            higher = tuple(b[:RANK] for b in both)
            return higher, better, squares(powers)

        def unfinished(state):
            return state[2] > 2e-6

        state = lax.while_loop(
            unfinished,
            improve,
            (tuple(seconds), tuple(eye + e for e in crossed), jnp.float32(1.0)),
        )
        for index, guess in enumerate(state[1]):
            scratch[index] = guess

    @pl.when(jnp.logical_not(close))
    def _():
        matrices = [eye - e for e in crossed]
        starts = []
        for matrix in matrices:
            level = jnp.abs(matrix)
            by_row = jnp.max(jnp.sum(level, 1, keepdims=True), 0, keepdims=True)
            by_column = jnp.max(jnp.sum(level, 0, keepdims=True), 1, keepdims=True)
            starts.append(matrix.T / by_row / by_column)

        def improve(state):
            count, _, guesses = state
            gaps = [eye - exact(m, g) for m, g in zip(matrices, guesses)]
            better = tuple(g + exact(g, gap) for g, gap in zip(guesses, gaps))
            return count + 1, squares(gaps), better

        def unfinished(state):
            count, error, _ = state
            return (count < 64) & jnp.logical_not(error <= 1e-7)

        state = lax.while_loop(
            unfinished, improve, (jnp.int32(0), jnp.float32(1.0), tuple(starts))
        )
        for index, guess in enumerate(state[2]):
            scratch[index] = guess


def merge(nodes, scratch, couples=()):
    crossed = [full(kb, ka) for ka, kb, _, _ in nodes]
    after = [c.shape[1] for c, _ in couples] or [0] * len(nodes)
    firsts = [[c] for c, _ in couples] or [[] for _ in nodes]
    shared = [
        exact(rb, jnp.concatenate(first + [ka], 1))
        for (ka, _, _, rb), first in zip(nodes, firsts)
    ]
    sides = [node[2] - both[:, at:] for node, both, at in zip(nodes, shared, after)]
    known = [both[:, :at] for both, at in zip(shared, after)]
    gains = [cb - exact(node[1], ca) for node, (ca, cb) in zip(nodes, couples)]
    inverses(crossed, scratch)
    bottoms = [exact(side, scratch[index]) for index, side in enumerate(sides)]
    seconds = [[gain] for gain in gains] or [[] for _ in nodes]
    applied = [
        exact(low, jnp.concatenate(second + [node[1]], 1))
        for low, second, node in zip(bottoms, seconds, nodes)
    ]
    tops = [node[3] - both[:, at:] for node, both, at in zip(nodes, applied, after)]
    updates = [first + both[:, :at] for first, both, at in zip(known, applied, after) if at]
    return tops, bottoms, updates


def tree(place, mine, other, out, first, second, third, whole, solved):
    first_core = place[5] == 0

    def rows(base, entry):
        parts = []
        for zh in range(4):
            here = pl.ds(base + entry * 4 + zh, 8, stride=MESSAGE)
            a, b = mine[here, :], other[here, :]
            parts += [jnp.where(first_core, a, b), jnp.where(first_core, b, a)]
        return jnp.concatenate(parts, 0)

    def left(values):
        return values[:, :RANK]

    def right(values):
        return values[:, RANK:]

    nodes = []
    couple = []
    carry = []
    for zl in range(4):
        xa, xb = rows(0, zl), rows(0, 4 + zl)
        fa, fb = rows(32, zl), rows(32, 4 + zl)
        nodes.append(
            (
                left(fa),
                left(fb),
                jnp.concatenate([left(xa), right(xa), right(fa)], 0),
                jnp.concatenate([left(xb), right(xb), right(fb)], 0),
            )
        )
        couple.append((rows(64, zl), rows(64, 4 + zl)))
        carry.append(jnp.concatenate([rows(96, zl), rows(112, zl), rows(128, zl)], 0))
    tops, bottoms, updates = merge(nodes, solved, couple)
    two = []
    one = []
    for zl in range(4):
        third[2 * zl] = tops[zl]
        third[2 * zl + 1] = bottoms[zl]
        carried = carry[zl] - updates[zl]
        two.append(left(carried))
        one.append(right(carried))

    def keep(values):
        return jnp.concatenate([values[:RANK], values[2 * RANK :]], 0)

    nodes = [
        (
            two[2 * m][RANK : 2 * RANK],
            two[2 * m + 1][RANK : 2 * RANK],
            keep(two[2 * m]),
            keep(two[2 * m + 1]),
        )
        for m in range(2)
    ]
    middle = [values[RANK : 2 * RANK] for values in one]
    tops, bottoms, updates = merge(nodes, solved, [middle[:2], middle[2:]])
    last = []
    for m in range(2):
        second[2 * m] = tops[m]
        second[2 * m + 1] = bottoms[m]
        last.append(keep(one[2 * m]) + keep(one[2 * m + 1]) - updates[m])
    node = (last[0][RANK:], last[1][RANK:], last[0][:RANK], last[1][:RANK])
    tops, bottoms, _ = merge([node], solved)
    first[0] = tops[0]
    first[1] = bottoms[0]

    zl, yh, zh = place[0], place[1], place[2]
    partner = place[3]
    target = place[4]
    c3 = third[2 * zl + yh]
    c2 = second[zl]
    d1 = first[zl // 2]
    d2 = c2[:RANK] - exact(d1, c2[RANK:])
    d3 = c3[:RANK] - exact(d2, c3[RANK : 2 * RANK]) - exact(d1, c3[2 * RANK :])
    whole[...] = jnp.concatenate([d3, d2, d1], 1)

    picked = jnp.concatenate(
        [whole[pl.ds(zh * 16, 16), :], whole[pl.ds(target * 16, 16), :]], 0
    )
    source = lax.broadcasted_iota(jnp.int32, (192, 128), 0)
    column = lax.broadcasted_iota(jnp.int32, (192, 128), 1)
    owner = jnp.where(column < 48, zh, partner)
    inner = jnp.where(column < 48, column, column - 48)
    wanted = (inner // 16) * RANK + owner * 16 + inner % 16
    out[32:, :] = jnp.zeros((96, 128), f32)
    out[:32, :] = -exact(picked, ((source == wanted) & (column < 96)).astype(f32))


def apply_rows(coefficient, *factors):
    high, low = split(coefficient)
    both = jnp.concatenate([high, low], 0)
    top, rest = split(jnp.concatenate([factor[...] for factor in factors], 0))
    wide = dot(both, top)
    return wide[:16] + (wide[16:] + dot(high, rest))


def outgoing(weights, own3, own, got3, got, out):
    out[...] = apply_rows(weights[16:32, :96], own3, own, got3, got)


def staying(weights, own3, own, got3, got, solves, out):
    out[...] = solves[...] + apply_rows(weights[0:16, :96], own3, own, got3, got)


def call(kernel, shapes, *arrays, scratch=(), **kwargs):
    return pl.pallas_call(
        kernel,
        out_shape=shapes,
        scratch_shapes=list(scratch),
        compiler_params=pltpu.CompilerParams(vmem_limit_bytes=LIMIT),
        cost_estimate=FREE,
        **kwargs,
    )(*arrays)


def shape(*dims):
    return jax.ShapeDtypeStruct(dims, f32)


def on_device(solves, factor3, factor2, factor1, basis3, basis2, basis1):
    zh = lax.axis_index("zh")
    core = lax.axis_index("core")
    near, far = zh ^ 1, 3 - zh
    place = jnp.stack(
        [
            lax.axis_index("zl"),
            lax.axis_index("yh"),
            zh,
            jnp.where(core == 0, near, far),
            jnp.where(core == 0, far, near),
            core,
        ]
    ).astype(jnp.int32)
    got3 = lax.ppermute(factor3, PAIRS, SWAP)
    slots, own = local_products(solves, factor3, factor2, factor1, basis3, basis2, basis1)
    slots = slots.reshape(16, 8, 128)
    slots, place = lax.optimization_barrier((slots, place))
    pieces = lax.all_to_all(slots, LEAF, 0, 0, tiled=True)
    vmem = pl.BlockSpec(memory_space=pltpu.VMEM)

    copies = call(leaf_sum, shape(32, 8, 128), pieces)
    copies, got3 = lax.optimization_barrier((copies, got3))
    slabs = lax.all_to_all(copies, SLAB, 0, 0, tiled=True)
    slabs, own = lax.optimization_barrier((slabs, own))
    got = lax.ppermute(own, PAIRS, SWAP)

    def solve():
        message = call(pack, shape(8, MESSAGE, 128), slabs)
        mine = lax.all_to_all(message, ("yl", "x"), 0, 0, tiled=True).reshape(8 * MESSAGE, 128)
        other = lax.ppermute(mine, "core", [(0, 1), (1, 0)])
        return call(
            tree,
            shape(128, 128),
            place,
            mine,
            other,
            in_specs=[pl.BlockSpec(memory_space=pltpu.SMEM), vmem, vmem],
            out_specs=vmem,
            scratch=[
                pltpu.VMEM((2, 64, 64), f32),
                pltpu.VMEM((4, 128, 64), f32),
                pltpu.VMEM((8, 192, 64), f32),
                pltpu.VMEM((64, 192), f32),
                pltpu.VMEM((4, 64, 64), f32),
            ],
        )

    once = lax.optimization_barrier(jnp.int32(1))
    coefficients = lax.cond(once > 0, solve, lambda: jnp.zeros((128, 128), f32))
    sent = call(outgoing, shape(16, ROWS), coefficients, factor3, own, got3, got)
    came = lax.ppermute(sent, PAIRS, RETURN)
    return call(staying, shape(16, ROWS), coefficients, factor3, own, got3, got, solves) + came


def solution(mesh):
    fine = Mesh(
        mesh.devices.reshape(4, 2, 2, 4, 2, 4), ("zl", "yh", "yl", "x", "core", "zh")
    )
    split_both = P("zh", BLOCKS)
    split_rows = P(None, BLOCKS)
    return jax.shard_map(
        on_device,
        mesh=fine,
        in_specs=(split_both,) * 4 + (split_rows,) * 3,
        out_specs=split_both,
        check_vma=False,
    )
```
